128 devices in a mesh: pos: 32 (over x, z, core), tile: 4 (over y).
Axes of the slice: x: 4, y: 4, z: 4, core: 2. Of those that a mesh axis runs over, the one named last changes fastest.
Arguments:
- object_slices: float32 [2, 2, 4096, 4096], P(None, None, 'pos', 'tile'), may hold values from -6 to 6
- probe: float32 [2, 256, 256], replicated, may hold values from -6 to 6
- patterns: float32 [128, 256, 256], P('pos'), may hold values from 0.25 to 4
- offsets: int32 [128, 2], P('pos'), may hold values from -128 to 896, as said below
- owner: int32 [128], P('pos'), may hold values from 0 to 3, as said below
Outputs:
- object_out: float32 [2, 2, 4096, 4096], P(None, None, 'pos', 'tile')
- probe_out: float32 [2, 256, 256], replicated
The draws below stay inside these ranges and needn't reach their ends.
Inputs may be any that keep to these rules, and one draw needn't show every extreme that they name: Among the 4 positions of a band at most 2 have the same owner, and in every band one owner has exactly 2. `offsets`: rows are relative to the band's first row, columns to the owner tile's first column; every patch lies inside the object.
All inputs are finite; a program needn't handle non-finite values.
Results may differ from the reference program's by a relative error of at most 0.03.
Values may be sent and summed in bfloat16 or wider, within the bound.
A program may use at most 128 MiB of HBM per device.

```python
import math
import jax
import jax.numpy as jnp
from jax import lax

WIN = 256
HALO = 128
NS = 2
ITERS = 2
BH = 128
BW = 1024
P_BAND = 4
MOST = 2
BANDS = 32
TILES = 4
NPOS = 128
OH = 4096
OW = 4096


def scan_layout(key):
    key_busy, key_rows, key_cols, key_other, key_perm = jax.random.split(key, 5)
    busy = jax.random.randint(key_busy, (BANDS,), 0, TILES)
    other = jax.random.randint(key_other, (BANDS, P_BAND), 1, TILES)
    slots = jnp.arange(P_BAND, dtype=jnp.int32)
    raw = jnp.where(slots[None, :] < MOST, busy[:, None], (busy[:, None] + other) % TILES)
    perm_keys = jax.random.split(key_perm, BANDS)
    orders = jax.vmap(lambda k: jax.random.permutation(k, P_BAND))(perm_keys)
    owners = jnp.take_along_axis(raw, orders, axis=1).reshape(-1).astype(jnp.int32)
    band_start = jnp.arange(NPOS, dtype=jnp.int32) // P_BAND * BH
    rel_rows = jax.random.randint(key_rows, (NPOS,), -HALO, BH - HALO + 1)
    rows = jnp.clip(band_start + rel_rows, 0, BH * BANDS - WIN) - band_start
    tile_start = owners * BW
    rel_cols = jax.random.randint(key_cols, (NPOS,), -HALO, BW - HALO + 1)
    cols = jnp.clip(tile_start + rel_cols, 0, BW * TILES - WIN) - tile_start
    offsets = jnp.stack([rows, cols], axis=1).astype(jnp.int32)
    return (owners, offsets)


def draw_offsets(key, part):
    owners, offsets = scan_layout(key)
    return offsets


def draw_owner(key, part):
    owners, offsets = scan_layout(key)
    return owners


def block_scale(stream_key, dims, cuts, smallest, high):
    def one(dim, blocks):
        steps = jax.random.uniform(jax.random.fold_in(jax.random.fold_in(stream_key, 6), dim), (blocks,), jnp.float32, smallest / len(cuts), high / len(cuts))
        return jnp.repeat(jnp.exp(steps), dims[dim] // blocks).reshape((-1,) + (1,) * (len(dims) - dim - 1))

    factor_of = one(*cuts[0])
    for cut in cuts[1:]:
        factor_of = factor_of * one(*cut)
    return factor_of


def centred(own_key, extent, scale, bound, pieces=(), kind=jnp.bfloat16):
    drawn = jax.random.normal(own_key, extent, jnp.float32) * scale
    if len(pieces) > 0:
        drawn = block_scale(own_key, extent, pieces, -0.22, 0.18) * drawn
    return jnp.clip(drawn, min=-bound, max=bound).astype(kind)


def setup_inputs(seed: int = 0) -> dict:
    key_of = jax.random.split(jax.random.key(seed), 6)
    return {
        "object_slices": centred(key_of[0], (NS, 2, OH, OW), 0.7, 6.0, ((2, 32), (3, 4)), jnp.float32),
        "probe": centred(key_of[1], (2, WIN, WIN), 1.0, 6.0, (), jnp.float32),
        "patterns": jnp.clip(jnp.exp(math.log(4.0) - 2.7725887 * jax.random.uniform(key_of[2], (NPOS, WIN, WIN), jnp.float32) ** block_scale(key_of[2], (NPOS, WIN, WIN), ((0, 32),), -0.2, 0.2)), 0.25, 4.0),
        "offsets": draw_offsets(jax.random.fold_in(key_of[5], 71), 0),
        "owner": draw_owner(jax.random.fold_in(key_of[5], 71), 0),
    }


fresnel = 0.05
eta_object = 0.5
eta_probe = 0.5

def dft_tables(width):
    indices = jnp.arange(width, dtype=jnp.int32)
    product = indices[:, None] * indices[None, :] % width
    angles = product.astype(jnp.float32) * (2.0 * math.pi / width)
    factor = 1.0 / math.sqrt(width)
    cosine = (jnp.cos(angles) * factor).astype(jnp.bfloat16)
    sines = (jnp.sin(angles) * factor).astype(jnp.bfloat16)
    frequency = ((indices + width // 2) % width - width // 2).astype(jnp.float32)
    phases = -math.pi * fresnel / width * (frequency[:, None] ** 2 + frequency[None, :] ** 2)
    kernel = jnp.stack([jnp.cos(phases), jnp.sin(phases)])
    return (cosine, sines, kernel)

def section(field, cosine, sines, sign, on_left):
    field32 = field.astype(jnp.float32)
    if on_left:
        cos_part = jnp.einsum('jk,sckl->scjl', cosine.astype(jnp.float32), field32, precision=lax.Precision.HIGHEST)
        sin_part = jnp.einsum('jk,sckl->scjl', sines.astype(jnp.float32), field32, precision=lax.Precision.HIGHEST)
    else:
        cos_part = jnp.einsum('scjk,kl->scjl', field32, cosine.astype(jnp.float32), precision=lax.Precision.HIGHEST)
        sin_part = jnp.einsum('scjk,kl->scjl', field32, sines.astype(jnp.float32), precision=lax.Precision.HIGHEST)
    real_part = cos_part[:, 0] + sign * sin_part[:, 1]
    imag_part = cos_part[:, 1] - sign * sin_part[:, 0]
    return jnp.stack([real_part, imag_part], axis=1)

def transform(field, tables, sign):
    cosine, sines, kernel = tables
    middle = section(field.astype(jnp.bfloat16), cosine, sines, sign, False).astype(jnp.bfloat16)
    return section(middle, cosine, sines, sign, True)

def complex_product(first, second):
    real_part = first[..., 0, :, :] * second[..., 0, :, :] - first[..., 1, :, :] * second[..., 1, :, :]
    imag_part = first[..., 0, :, :] * second[..., 1, :, :] + first[..., 1, :, :] * second[..., 0, :, :]
    return jnp.stack([real_part, imag_part], axis=-3)

def conjugate_product(first, second):
    real_part = first[..., 0, :, :] * second[..., 0, :, :] + first[..., 1, :, :] * second[..., 1, :, :]
    imag_part = first[..., 0, :, :] * second[..., 1, :, :] - first[..., 1, :, :] * second[..., 0, :, :]
    return jnp.stack([real_part, imag_part], axis=-3)

def position_gradients(probe, patches, patterns, tables):
    slices = patches.astype(jnp.float32)
    count = slices.shape[1]
    kernel = tables[2]
    incoming = jnp.broadcast_to(probe, (slices.shape[0],) + probe.shape)
    waves = []
    leaving = incoming
    for level in range(count):
        waves.append(incoming)
        leaving = complex_product(incoming, slices[:, level])
        if level + 1 < count:
            incoming = transform(complex_product(kernel, transform(leaving, tables, 1.0)), tables, -1.0)
    farfield = transform(leaving, tables, 1.0)
    power = farfield[:, 0] ** 2 + farfield[:, 1] ** 2
    misfit = (power - patterns)[:, None] * farfield
    backward = transform(misfit, tables, -1.0)
    slice_grads = [None] * count
    upstream = backward
    for level in reversed(range(count)):
        slice_grads[level] = conjugate_product(waves[level], backward)
        upstream = conjugate_product(slices[:, level], backward)
        if level > 0:
            backward = transform(conjugate_product(kernel, transform(upstream, tables, 1.0)), tables, -1.0)
    return (jnp.stack(slice_grads, axis=1), upstream)

def reference(object_slices, probe, patterns, offsets, owner):
    tables = dft_tables(WIN)
    zero = jnp.zeros((), jnp.int32)
    band_start = jnp.arange(NPOS, dtype=jnp.int32) // P_BAND * BH
    corner_rows = (band_start + offsets[:, 0]).astype(jnp.int32).reshape(BANDS, P_BAND)
    corner_cols = (owner * BW + offsets[:, 1]).astype(jnp.int32).reshape(BANDS, P_BAND)
    band_patterns = patterns.reshape(BANDS, P_BAND, WIN, WIN)
    field = object_slices
    current = probe
    for sweep in range(ITERS):
        lowered = field.astype(jnp.bfloat16)

        def one_band(carry, inputs):
            grad_sum, probe_sum = carry
            these_patterns, these_rows, these_cols = inputs
            patches = jax.vmap(lambda r, c: lax.dynamic_slice(lowered, (zero, zero, r, c), (NS, 2, WIN, WIN)))(these_rows, these_cols)
            slice_grads, probe_grads = position_gradients(current, patches, these_patterns, tables)
            probe_sum = probe_sum + lax.optimization_barrier(jnp.sum(probe_grads, axis=0))

            def add_one(k, total):
                start = (zero, zero, these_rows[k], these_cols[k])
                before = lax.dynamic_slice(total, start, (NS, 2, WIN, WIN))
                return lax.dynamic_update_slice(total, before + slice_grads[k], start)
            grad_sum = lax.fori_loop(0, P_BAND, add_one, grad_sum)
            return ((grad_sum, probe_sum), None)
        start_carry = (jnp.zeros(field.shape, jnp.float32), jnp.zeros((2, WIN, WIN), jnp.float32))
        (grad_sum, probe_sum), _ = lax.scan(one_band, start_carry, (band_patterns, corner_rows, corner_cols))
        mean_square = jnp.sum(grad_sum * grad_sum) / float(NS * 2 * OH * OW)
        field = field - eta_object * lax.rsqrt(mean_square + 1e-06) * grad_sum
        probe_square = jnp.sum(probe_sum * probe_sum) / float(2 * WIN * WIN)
        current = current - eta_probe * lax.rsqrt(probe_square + 1e-06) * probe_sum
    return (field, current)
```

```python
import functools
import math

import jax
import jax.numpy as jnp
import numpy as np
from jax import lax
from jax.experimental import pallas as pl
from jax.experimental.pallas import tpu as pltpu
from jax.sharding import PartitionSpec as P

ITERS = 2
MOST = 2
FRESNEL = 0.05
ETA_OBJECT = 0.5
ETA_PROBE = 0.5
W = 256
M = 128
MESH = pl.DeviceIdType.MESH
F32 = jnp.float32
BF16 = jnp.bfloat16


def tables():
    indices = np.arange(W)
    angles = (indices[:, None] * indices[None, :] % W) * (2.0 * math.pi / W)
    cosine = np.cos(angles) / math.sqrt(W)
    sine = np.sin(angles) / math.sqrt(W)
    ahead = np.block([[cosine, -sine], [sine, cosine]])
    behind = np.block([[cosine, sine], [-sine, cosine]])
    dft = np.stack([ahead, behind]).astype(np.float32).astype(jnp.bfloat16)
    frequency = ((indices + W // 2) % W - W // 2).astype(np.float32)
    phases = -math.pi * FRESNEL / W * (frequency[:, None] ** 2 + frequency[None, :] ** 2)
    spread = np.stack([np.cos(phases), np.sin(phases)]).astype(np.float32)
    return dft, spread


def slot_info(owner_of, offset_of, bands, tile):
    zero = jnp.int32(0)
    found = zero
    slots = [[zero, zero, zero, zero] for _ in range(MOST)]
    for n in range(bands):
        live = owner_of(n) == tile
        row, col = offset_of(n, 0) + M, offset_of(n, 1) + M
        for k in range(MOST):
            here = jnp.logical_and(live, found == k)
            slots[k] = [
                jnp.where(here, new, old)
                for new, old in zip((row, col, jnp.int32(n), jnp.int32(1)), slots[k])
            ]
        found = found + live.astype(jnp.int32)
    return slots


def one_hot(rows, cols, shift):
    row = lax.broadcasted_iota(jnp.int32, (rows, cols), 0)
    col = lax.broadcasted_iota(jnp.int32, (rows, cols), 1)
    return (row == col + shift).astype(F32).astype(BF16)


def dot(a, b):
    return jnp.dot(a, b, preferred_element_type=F32)


def body(sizes, *refs):
    (npos, ntile, nw, bands, block_cols, cells) = sizes
    (off, own, obj, probe_in, pats_in, tab_in, spread_in, obj_out, probe_out) = refs[:9]
    (
        off_nb, own_nb, fld, acc, low, parts, halo_send, fold_send, contrib, edge_send, edge_recv,
        probe, pats, tab, spread, place, rows_in, rows_out, patch, x, mid, psi1, pg,
        rs1_send, rs1, rs2_send, rs2, ag_send, ag, sq_a, sq_b, sq_sa, sq_sb,
        local_sem, info_s, info_r, col_s, col_r, halo_s, halo_r, fold_s, fold_r, edge_s, edge_r,
        p_s, p_r, q_s, q_r,
    ) = refs[9:]
    grown = block_cols + 2 * M
    nx = npos // nw
    ng = nx * ntile
    p = lax.axis_index("pos")
    t = lax.axis_index("tile")
    xi, wi = p // nw, p % nw
    me_g = xi * ntile + t

    up = {"pos": lax.rem(p + npos - 1, npos)}
    down = {"pos": lax.rem(p + 1, npos)}
    left = {"tile": lax.rem(t + ntile - 1, ntile)}
    right = {"tile": lax.rem(t + 1, ntile)}

    def g_peer(j):
        return {
            "pos": lax.rem(xi + j // ntile, nx) * nw + wi,
            "tile": lax.rem(t + j % ntile, ntile),
        }

    def g_index(j):
        return lax.rem(xi + j // ntile, nx) * ntile + lax.rem(t + j % ntile, ntile)

    def w_peer(j):
        return {"pos": xi * nw + lax.rem(wi + j, nw)}

    def remote(src, dst, send, recv, where):
        return pltpu.make_async_remote_copy(
            src_ref=src, dst_ref=dst, send_sem=send, recv_sem=recv, device_id=where, device_id_type=MESH
        )

    def wait_bytes(ref, sem):
        pltpu.make_async_copy(ref, ref, sem).wait()

    loads = [
        pltpu.make_async_copy(obj, fld.at[:, :, pl.ds(M, block_cols)], local_sem.at[0]),
        pltpu.make_async_copy(probe_in, probe, local_sem.at[1]),
        pltpu.make_async_copy(tab_in, tab, local_sem.at[2]),
        pltpu.make_async_copy(spread_in, spread, local_sem.at[3]),
        pltpu.make_async_copy(pats_in, pats, local_sem.at[4]),
    ]
    for load in loads:
        load.start()

    barrier = pltpu.get_barrier_semaphore()
    friends = [up, down, left, right]
    friends += [g_peer(j) for j in range(1, ng)]
    friends += [w_peer(j) for j in range(1, nw)]
    for friend in friends:
        pl.semaphore_signal(barrier, inc=1, device_id=friend, device_id_type=MESH)
    pl.semaphore_wait(barrier, len(friends))

    info = [
        remote(off, off_nb.at[0], info_s.at[0], info_r.at[0], down),
        remote(own, own_nb.at[0], info_s.at[1], info_r.at[1], down),
        remote(off, off_nb.at[1], info_s.at[2], info_r.at[2], up),
        remote(own, own_nb.at[1], info_s.at[3], info_r.at[3], up),
    ]
    cols = [
        remote(obj.at[:, :, pl.ds(block_cols - M, M)], fld.at[:, :, pl.ds(0, M)], col_s.at[0], col_r.at[0], right),
        remote(obj.at[:, :, pl.ds(0, M)], fld.at[:, :, pl.ds(M + block_cols, M)], col_s.at[1], col_r.at[1], left),
    ]
    for copy in info + cols:
        copy.start()

    mine = slot_info(lambda n: own[n], lambda n, i: off[n, i], bands, t)
    for k in range(MOST):
        rows_in[k] = (
            lax.broadcasted_iota(jnp.int32, (W, 3 * M), 1)
            == lax.broadcasted_iota(jnp.int32, (W, 3 * M), 0) + mine[k][0]
        ).astype(F32).astype(BF16)
        rows_out[k] = one_hot(3 * M, W, mine[k][0])
    for copy in info:
        copy.wait_recv()
    above = slot_info(lambda n: own_nb[0, n], lambda n, i: off_nb[0, n, i], bands, t)
    below = slot_info(lambda n: own_nb[1, n], lambda n, i: off_nb[1, n, i], bands, t)
    slots = above + mine + below
    for k in range(3 * MOST):
        place[pl.ds(k * W, W), :] = (
            lax.broadcasted_iota(jnp.int32, (W, grown), 1)
            == lax.broadcasted_iota(jnp.int32, (W, grown), 0) + slots[k][1]
        ).astype(F32).astype(BF16)
    for copy in cols:
        copy.wait_recv()
    for load in loads:
        load.wait()

    sends = info + cols

    def transform(k, way):
        half = dot(x[k], tab[way]).astype(BF16)
        mid[k, pl.ds(0, W)] = half[:, :W]
        mid[k, pl.ds(W, W)] = half[:, W:]
        both = dot(tab[1 - way], mid[k])
        return both[:W], both[W:]

    def put(k, re, im):
        x[k, :, pl.ds(0, W)] = re.astype(BF16)
        x[k, :, pl.ds(W, W)] = im.astype(BF16)

    for it in range(ITERS):
        low[...] = fld[...].astype(BF16)

        def chosen(k):
            return lax.dot_general(
                low[...].reshape(4 * M, grown),
                place[pl.ds(k * W, W), :],
                (((1,), (1,)), ((), ())),
                preferred_element_type=F32,
            ).astype(BF16).reshape(4, M, W)

        for k in range(MOST):
            halo_send[it, 0, k] = chosen(k)
            halo_send[it, 1, k] = chosen(2 * MOST + k)
        halo = [
            remote(halo_send.at[it, 0], parts.at[it, 2], halo_s.at[it, 0], halo_r.at[it, 0], up),
            remote(halo_send.at[it, 1], parts.at[it, 0], halo_s.at[it, 1], halo_r.at[it, 1], down),
        ]
        for copy in halo:
            copy.start()
        sends += halo
        for k in range(MOST):
            parts[it, 1, k] = chosen(MOST + k)
        for copy in halo:
            copy.wait_recv()
        for k in range(MOST):
            for c in range(4):
                stack = jnp.concatenate([parts[it, 0, k, c], parts[it, 1, k, c], parts[it, 2, k, c]], axis=0)
                patch[k, c] = dot(rows_in[k], stack)

        for k in range(MOST):
            re = probe[0] * patch[k, 0] - probe[1] * patch[k, 1]
            im = probe[0] * patch[k, 1] + probe[1] * patch[k, 0]
            put(k, re, im)
        for k in range(MOST):
            a, b = transform(k, 0)
            put(k, spread[0] * a - spread[1] * b, spread[0] * b + spread[1] * a)
        for k in range(MOST):
            a, b = transform(k, 1)
            psi1[k, 0] = a
            psi1[k, 1] = b
            put(k, a * patch[k, 2] - b * patch[k, 3], a * patch[k, 3] + b * patch[k, 2])
        for k in range(MOST):
            a, b = transform(k, 0)
            wanted = jnp.zeros((W, W), F32)
            for n in range(bands):
                wanted = jnp.where(mine[k][2] == n, pats[n], wanted)
            misfit = a * a + b * b - wanted
            put(k, misfit * a, misfit * b)

        def fold_out(k, c, value):
            value = jnp.where(mine[k][3] > 0, value, 0.0).astype(BF16)
            rows = dot(rows_out[k], value).astype(BF16)
            fold_send[it, 0, k, c] = rows[:M]
            contrib[it, 1, k, c] = rows[M : 2 * M]
            fold_send[it, 1, k, c] = rows[2 * M :]

        for k in range(MOST):
            a, b = transform(k, 1)
            put(k, patch[k, 2] * a + patch[k, 3] * b, patch[k, 2] * b - patch[k, 3] * a)
            fold_out(k, 2, psi1[k, 0] * a + psi1[k, 1] * b)
            fold_out(k, 3, psi1[k, 0] * b - psi1[k, 1] * a)
        for k in range(MOST):
            a, b = transform(k, 0)
            put(k, spread[0] * a + spread[1] * b, spread[0] * b - spread[1] * a)
        for k in range(MOST):
            a, b = transform(k, 1)
            fold_out(k, 0, probe[0] * a + probe[1] * b)
            fold_out(k, 1, probe[0] * b - probe[1] * a)
            re = jnp.where(mine[k][3] > 0, patch[k, 0] * a + patch[k, 1] * b, 0.0)
            im = jnp.where(mine[k][3] > 0, patch[k, 0] * b - patch[k, 1] * a, 0.0)
            if k == 0:
                pg[pl.ds(0, W)] = re
                pg[pl.ds(W, W)] = im
            else:
                pg[pl.ds(0, W)] = pg[pl.ds(0, W)] + re
                pg[pl.ds(W, W)] = pg[pl.ds(W, W)] + im

        fold = [
            remote(fold_send.at[it, 0], contrib.at[it, 2], fold_s.at[it, 0], fold_r.at[it, 0], up),
            remote(fold_send.at[it, 1], contrib.at[it, 0], fold_s.at[it, 1], fold_r.at[it, 1], down),
        ]
        for copy in fold:
            copy.start()
        sends += fold
        chunk = 2 * W // ng
        rs1_send[it] = pg[...].astype(BF16).reshape(ng, chunk, W)
        for j in range(1, ng):
            remote(
                rs1_send.at[it, g_index(j)], rs1.at[it, me_g], p_s.at[it, 0], p_r.at[it, 0], g_peer(j)
            ).start()
        rs1[it, me_g] = rs1_send[it, me_g]

        for copy in fold:
            copy.wait_recv()
        terms = jnp.concatenate(
            [contrib[it, s, k].reshape(4 * M, W) for s in range(3) for k in range(MOST)], axis=1
        )
        for start in (0, grown - W):
            acc[:, :, pl.ds(start, W)] = dot(terms, place[:, pl.ds(start, W)]).reshape(4, M, W)
        edge_send[it, 0] = acc[:, :, pl.ds(0, W)].astype(BF16)
        edge_send[it, 1] = acc[:, :, pl.ds(grown - W, W)].astype(BF16)
        edge = [
            remote(edge_send.at[it, 0], edge_recv.at[it, 1], edge_s.at[it, 0], edge_r.at[it, 0], left),
            remote(edge_send.at[it, 1], edge_recv.at[it, 0], edge_s.at[it, 1], edge_r.at[it, 1], right),
        ]
        for copy in edge:
            copy.start()
        sends += edge
        for start in range(W, grown - W, W):
            acc[:, :, pl.ds(start, W)] = dot(terms, place[:, pl.ds(start, W)]).reshape(4, M, W)

        wait_bytes(rs1.at[it, pl.ds(0, ng - 1)], p_r.at[it, 0])
        rs2_send[it] = jnp.sum(rs1[it].astype(F32), axis=0).astype(BF16)
        for j in range(1, nw):
            remote(rs2_send.at[it], rs2.at[it, wi], p_s.at[it, 1], p_r.at[it, 1], w_peer(j)).start()
        rs2[it, wi] = rs2_send[it]

        for copy in edge:
            copy.wait_recv()
        acc[:, :, pl.ds(0, W)] = acc[:, :, pl.ds(0, W)] + edge_recv[it, 0].astype(F32)
        acc[:, :, pl.ds(grown - W, W)] = acc[:, :, pl.ds(grown - W, W)] + edge_recv[it, 1].astype(F32)
        inner = acc[:, :, pl.ds(M, block_cols)].reshape(4 * M, block_cols)
        squares = jnp.sum((inner * inner).reshape(4 * M // 8, 8, block_cols), axis=0)
        total = squares[:, :M]
        for i in range(1, block_cols // M):
            total = total + squares[:, i * M : (i + 1) * M]
        sq_sa[it] = total
        for j in range(1, ng):
            remote(sq_sa.at[it], sq_a.at[it, me_g], q_s.at[it, 0], q_r.at[it, 0], g_peer(j)).start()
        sq_a[it, me_g] = sq_sa[it]

        wait_bytes(rs2.at[it, pl.ds(0, nw - 1)], p_r.at[it, 1])
        ag_send[it] = jnp.sum(rs2[it].astype(F32), axis=0).astype(BF16)
        for j in range(1, ng):
            remote(ag_send.at[it], ag.at[it, me_g], p_s.at[it, 2], p_r.at[it, 2], g_peer(j)).start()
        ag[it, me_g] = ag_send[it]

        wait_bytes(sq_a.at[it, pl.ds(0, ng - 1)], q_r.at[it, 0])
        sq_sb[it] = jnp.sum(sq_a[it], axis=0)
        for j in range(1, nw):
            remote(sq_sb.at[it], sq_b.at[it, wi], q_s.at[it, 1], q_r.at[it, 1], w_peer(j)).start()
        sq_b[it, wi] = sq_sb[it]

        wait_bytes(ag.at[it, pl.ds(0, ng - 1)], p_r.at[it, 2])
        grad = ag[it].astype(F32).reshape(2, W, W)
        mean = jnp.sum(grad * grad) / float(2 * W * W)
        probe[...] = probe[...] - ETA_PROBE * lax.rsqrt(mean + 1e-06) * grad

        wait_bytes(sq_b.at[it, pl.ds(0, nw - 1)], q_r.at[it, 1])
        mean = jnp.sum(jnp.sum(sq_b[it], axis=0)) / cells
        fld[...] = fld[...] - ETA_OBJECT * lax.rsqrt(mean + 1e-06) * acc[...]

    stores = [
        pltpu.make_async_copy(fld.at[:, :, pl.ds(M, block_cols)], obj_out, local_sem.at[0]),
        pltpu.make_async_copy(probe, probe_out, local_sem.at[1]),
    ]
    for store in stores:
        store.start()
    for copy in sends:
        copy.wait_send()
    for it in range(ITERS):
        wait_bytes(rs1_send.at[it, pl.ds(0, ng - 1)], p_s.at[it, 0])
        wait_bytes(rs2.at[it, pl.ds(0, nw - 1)], p_s.at[it, 1])
        wait_bytes(ag.at[it, pl.ds(0, ng - 1)], p_s.at[it, 2])
        wait_bytes(sq_a.at[it, pl.ds(0, ng - 1)], q_s.at[it, 0])
        wait_bytes(sq_b.at[it, pl.ds(0, nw - 1)], q_s.at[it, 1])
    for store in stores:
        store.wait()


def per_device(object_slices, probe, patterns, offsets, owner):
    nslice, _, rows, cols = object_slices.shape
    bands = patterns.shape[0]
    npos, ntile = lax.axis_size("pos"), lax.axis_size("tile")
    nw = 8 if npos % 8 == 0 else 2
    ng = npos // nw * ntile
    chunk = 2 * W // ng
    grown = cols + 2 * M
    cells = float(nslice * 2 * rows * cols * npos * ntile)
    dft, spread = tables()
    vmem, dma = pltpu.VMEM, pltpu.SemaphoreType.DMA
    any_space = pl.BlockSpec(memory_space=pl.ANY)
    smem_space = pl.BlockSpec(memory_space=pltpu.SMEM)
    scratch = [
        pltpu.SMEM((2, bands, 2), jnp.int32),
        pltpu.SMEM((2, bands), jnp.int32),
        vmem((4, M, grown), F32),
        vmem((4, M, grown), F32),
        vmem((4, M, grown), BF16),
        vmem((ITERS, 3, MOST, 4, M, W), BF16),
        vmem((ITERS, 2, MOST, 4, M, W), BF16),
        vmem((ITERS, 2, MOST, 4, M, W), BF16),
        vmem((ITERS, 3, MOST, 4, M, W), BF16),
        vmem((ITERS, 2, 4, M, W), BF16),
        vmem((ITERS, 2, 4, M, W), BF16),
        vmem((2, W, W), F32),
        vmem((bands, W, W), F32),
        vmem((2, 2 * W, 2 * W), BF16),
        vmem((2, W, W), F32),
        vmem((3 * MOST * W, grown), BF16),
        vmem((MOST, W, 3 * M), BF16),
        vmem((MOST, 3 * M, W), BF16),
        vmem((MOST, 4, W, W), F32),
        vmem((MOST, W, 2 * W), BF16),
        vmem((MOST, 2 * W, W), BF16),
        vmem((MOST, 2, W, W), F32),
        vmem((2 * W, W), F32),
        vmem((ITERS, ng, chunk, W), BF16),
        vmem((ITERS, ng, chunk, W), BF16),
        vmem((ITERS, chunk, W), BF16),
        vmem((ITERS, nw, chunk, W), BF16),
        vmem((ITERS, chunk, W), BF16),
        vmem((ITERS, ng, chunk, W), BF16),
        vmem((ITERS, ng, 8, M), F32),
        vmem((ITERS, nw, 8, M), F32),
        vmem((ITERS, 8, M), F32),
        vmem((ITERS, 8, M), F32),
        dma((5,)),
        dma((4,)), dma((4,)),
        dma((2,)), dma((2,)),
        dma((ITERS, 2)), dma((ITERS, 2)),
        dma((ITERS, 2)), dma((ITERS, 2)),
        dma((ITERS, 2)), dma((ITERS, 2)),
        dma((ITERS, 3)), dma((ITERS, 3)),
        dma((ITERS, 2)), dma((ITERS, 2)),
    ]
    field, current = pl.pallas_call(
        functools.partial(body, (npos, ntile, nw, bands, cols, cells)),
        out_shape=(
            jax.ShapeDtypeStruct((4, rows, cols), F32),
            jax.ShapeDtypeStruct((2, W, W), F32),
        ),
        in_specs=[smem_space] * 2 + [any_space] * 5,
        out_specs=(any_space, any_space),
        scratch_shapes=scratch,
        compiler_params=pltpu.CompilerParams(
            collective_id=0, has_side_effects=True, vmem_limit_bytes=56 * 1024 * 1024
        ),
    )(
        offsets,
        owner,
        object_slices.reshape(4, rows, cols),
        probe,
        patterns,
        jnp.asarray(dft),
        jnp.asarray(spread),
    )
    return field.reshape(nslice, 2, rows, cols), current


def solution(mesh):
    return jax.shard_map(
        per_device,
        mesh=mesh,
        in_specs=(
            P(None, None, "pos", "tile"),
            P(),
            P("pos", None, None),
            P("pos", None),
            P("pos"),
        ),
        out_specs=(P(None, None, "pos", "tile"), P()),
        check_vma=False,
    )
```

```python
import functools
import math

import jax
import jax.numpy as jnp
import numpy as np
from jax import lax
from jax.experimental import pallas as pl
from jax.experimental.pallas import tpu as pltpu
from jax.sharding import PartitionSpec as P

ITERS = 2
MOST = 2
FRESNEL = 0.05
ETA_OBJECT = 0.5
ETA_PROBE = 0.5
W = 256
M = 128
MESH = pl.DeviceIdType.MESH
F32 = jnp.float32
BF16 = jnp.bfloat16


def tables():
    indices = np.arange(W)
    angles = (indices[:, None] * indices[None, :] % W) * (2.0 * math.pi / W)
    cosine = np.cos(angles) / math.sqrt(W)
    sine = np.sin(angles) / math.sqrt(W)
    ahead = np.block([[cosine, -sine], [sine, cosine]])
    behind = np.block([[cosine, sine], [-sine, cosine]])
    dft = np.stack([ahead, behind]).astype(np.float32).astype(jnp.bfloat16)
    frequency = ((indices + W // 2) % W - W // 2).astype(np.float32)
    phases = -math.pi * FRESNEL / W * (frequency[:, None] ** 2 + frequency[None, :] ** 2)
    spread = np.stack([np.cos(phases), np.sin(phases)]).astype(np.float32)
    return dft, spread


def slot_info(owner_of, offset_of, bands, tile):
    zero = jnp.int32(0)
    found = zero
    slots = [[zero, zero, zero, zero] for _ in range(MOST)]
    for n in range(bands):
        live = owner_of(n) == tile
        row, col = offset_of(n, 0) + M, offset_of(n, 1) + M
        for k in range(MOST):
            here = jnp.logical_and(live, found == k)
            slots[k] = [
                jnp.where(here, new, old)
                for new, old in zip((row, col, jnp.int32(n), jnp.int32(1)), slots[k])
            ]
        found = found + live.astype(jnp.int32)
    return slots


def one_hot(rows, cols, shift):
    row = lax.broadcasted_iota(jnp.int32, (rows, cols), 0)
    col = lax.broadcasted_iota(jnp.int32, (rows, cols), 1)
    return (row == col + shift).astype(F32).astype(BF16)


def dot(a, b):
    return jnp.dot(a, b, preferred_element_type=F32)


def body(sizes, *refs):
    (npos, ntile, nw, bands, block_cols, cells) = sizes
    (off_in, own_in, obj, probe_in, pats_in, tab_in, spread_in, obj_out, probe_out) = refs[:9]
    (
        off, own, off_nb, own_nb, fld, acc, low, steps, parts, halo_send, fold_send, contrib, edge_send, edge_recv,
        probe, pats, wanted, tab, spread, place, rows_in, rows_out, patch, x, mid, psi1, pg,
        rs1_send, rs1, rs2_send, rs2, ag_send, ag, sq_a, sq_b, sq_sa, sq_sb,
        local_sem, info_s, info_r, col_s, col_r, halo_s, halo_r, fold_s, fold_r, edge_s, edge_r,
        p_s, p_r, q_s, q_r,
    ) = refs[9:]
    grown = block_cols + 2 * M
    nx = npos // nw
    ng = nx * ntile
    chunk = 2 * W // ng
    p = lax.axis_index("pos")
    t = lax.axis_index("tile")
    xi, wi = p // nw, p % nw
    me_g = xi * ntile + t

    up = {"pos": lax.rem(p + npos - 1, npos)}
    down = {"pos": lax.rem(p + 1, npos)}
    left = {"tile": lax.rem(t + ntile - 1, ntile)}
    right = {"tile": lax.rem(t + 1, ntile)}

    def g_peer(j):
        return {
            "pos": lax.rem(xi + j // ntile, nx) * nw + wi,
            "tile": lax.rem(t + j % ntile, ntile),
        }

    def g_index(j):
        return lax.rem(xi + j // ntile, nx) * ntile + lax.rem(t + j % ntile, ntile)

    def w_peer(j):
        return {"pos": xi * nw + lax.rem(wi + j, nw)}

    def remote(src, dst, send, recv, where):
        return pltpu.make_async_remote_copy(
            src_ref=src, dst_ref=dst, send_sem=send, recv_sem=recv, device_id=where, device_id_type=MESH
        )

    def wait_bytes(ref, sem):
        pltpu.make_async_copy(ref, ref, sem).wait()

    loads = [
        pltpu.make_async_copy(off_in, off, local_sem.at[0]),
        pltpu.make_async_copy(own_in, own, local_sem.at[1]),
        pltpu.make_async_copy(obj, fld, local_sem.at[2]),
        pltpu.make_async_copy(pats_in, pats, local_sem.at[3]),
        pltpu.make_async_copy(probe_in, probe, local_sem.at[4]),
        pltpu.make_async_copy(tab_in, tab, local_sem.at[5]),
        pltpu.make_async_copy(spread_in, spread, local_sem.at[6]),
    ]
    for load in loads:
        load.start()

    barrier = pltpu.get_barrier_semaphore()
    friends = [up, down, left, right]
    friends += [g_peer(j) for j in range(1, ng)]
    friends += [w_peer(j) for j in range(1, nw)]
    for friend in friends:
        pl.semaphore_signal(barrier, inc=1, device_id=friend, device_id_type=MESH)
    for load in loads[:3]:
        load.wait()
    low[:, :, pl.ds(M, block_cols)] = fld[...].astype(BF16)
    pl.semaphore_wait(barrier, len(friends))

    info = [
        remote(off, off_nb.at[0], info_s.at[0], info_r.at[0], down),
        remote(own, own_nb.at[0], info_s.at[1], info_r.at[1], down),
        remote(off, off_nb.at[1], info_s.at[2], info_r.at[2], up),
        remote(own, own_nb.at[1], info_s.at[3], info_r.at[3], up),
    ]
    for copy in info:
        copy.start()
    cols = []
    for s in range(2):
        rows = pl.ds(2 * s, 2)
        cols.append([
            remote(
                low.at[rows, :, pl.ds(block_cols, M)], low.at[rows, :, pl.ds(0, M)],
                col_s.at[s, 0], col_r.at[s, 0], right,
            ),
            remote(
                low.at[rows, :, pl.ds(M, M)], low.at[rows, :, pl.ds(M + block_cols, M)],
                col_s.at[s, 1], col_r.at[s, 1], left,
            ),
        ])
        for copy in cols[s]:
            copy.start()
    sends = info + cols[0] + cols[1]

    def build_place(k, slot):
        place[pl.ds(k * W, W), :] = (
            lax.broadcasted_iota(jnp.int32, (W, grown), 1)
            == lax.broadcasted_iota(jnp.int32, (W, grown), 0) + slot[1]
        ).astype(F32).astype(BF16)

    mine = slot_info(lambda n: own[n], lambda n, i: off[n, i], bands, t)
    for k in range(MOST):
        rows_in[k] = (
            lax.broadcasted_iota(jnp.int32, (W, 3 * M), 1)
            == lax.broadcasted_iota(jnp.int32, (W, 3 * M), 0) + mine[k][0]
        ).astype(F32).astype(BF16)
        rows_out[k] = one_hot(3 * M, W, mine[k][0])
        build_place(MOST + k, mine[k])
    for copy in info:
        copy.wait_recv()
    above = slot_info(lambda n: own_nb[0, n], lambda n, i: off_nb[0, n, i], bands, t)
    below = slot_info(lambda n: own_nb[1, n], lambda n, i: off_nb[1, n, i], bands, t)
    for k in range(MOST):
        build_place(k, above[k])
        build_place(2 * MOST + k, below[k])

    def chosen(source, s, group):
        return lax.dot_general(
            source[pl.ds(2 * s, 2)].reshape(2 * M, grown),
            place[pl.ds(group * MOST * W, MOST * W), :],
            (((1,), (1,)), ((), ())),
            preferred_element_type=F32,
        ).astype(BF16)

    def start_halo(h, s, source):
        copies = []
        for way, (group, part, where) in enumerate(((0, 2, up), (2, 0, down))):
            columns = chosen(source, s, group)
            for k in range(MOST):
                halo_send[h, way, s, k] = columns[:, k * W : (k + 1) * W].reshape(2, M, W)
            copy = remote(
                halo_send.at[h, way, s], parts.at[h, part, s], halo_s.at[h, s, way], halo_r.at[h, s, way], where
            )
            copy.start()
            copies.append(copy)
        return copies

    def own_columns(h, s, source):
        columns = chosen(source, s, 1)
        for k in range(MOST):
            parts[h, 1, s, k] = columns[:, k * W : (k + 1) * W].reshape(2, M, W)

    def window(h, s, k, c):
        stack = jnp.concatenate([parts[h, 0, s, k, c], parts[h, 1, s, k, c], parts[h, 2, s, k, c]], axis=0)
        return dot(rows_in[k], stack)

    halo = []
    for s in range(2):
        for copy in cols[s]:
            copy.wait_recv()
        halo.append(start_halo(0, s, low))
    for s in range(2):
        own_columns(0, s, low)
    for load in loads[3:]:
        load.wait()
    for k in range(MOST):
        found = pats[0]
        for n in range(1, bands):
            found = jnp.where(mine[k][2] == n, pats[n], found)
        wanted[k] = found

    def transform(k, way):
        half = dot(x[k], tab[way]).astype(BF16)
        mid[k, pl.ds(0, W)] = half[:, :W]
        mid[k, pl.ds(W, W)] = half[:, W:]
        both = dot(tab[1 - way], mid[k])
        return both[:W], both[W:]

    def put(k, re, im):
        x[k, :, pl.ds(0, W)] = re.astype(BF16)
        x[k, :, pl.ds(W, W)] = im.astype(BF16)

    for it in range(ITERS):

        def fold_out(k, s, c, value):
            rows = dot(rows_out[k], value.astype(BF16)).astype(BF16)
            fold_send[it, 0, s, k, c] = rows[:M]
            contrib[it, 1, s, k, c] = rows[M : 2 * M]
            fold_send[it, 1, s, k, c] = rows[2 * M :]

        def start_fold(s):
            copies = [
                remote(
                    fold_send.at[it, 0, s], contrib.at[it, 2, s], fold_s.at[it, s, 0], fold_r.at[it, s, 0], up
                ),
                remote(
                    fold_send.at[it, 1, s], contrib.at[it, 0, s], fold_s.at[it, s, 1], fold_r.at[it, s, 1], down
                ),
            ]
            for copy in copies:
                copy.start()
            return copies

        def sum_columns(terms, s, start):
            acc[pl.ds(2 * s, 2), :, pl.ds(start, W)] = dot(terms, place[:, pl.ds(start, W)]).reshape(2, M, W)

        def sum_slice(s):
            terms = jnp.concatenate(
                [contrib[it, g, s, k].reshape(2 * M, W) for g in range(3) for k in range(MOST)], axis=1
            )
            copies = []
            for way, (start, where) in enumerate(((0, left), (grown - W, right))):
                sum_columns(terms, s, start)
                edge_send[it, way, s] = acc[pl.ds(2 * s, 2), :, pl.ds(start, W)].astype(BF16)
                copy = remote(
                    edge_send.at[it, way, s], edge_recv.at[it, 1 - way, s],
                    edge_s.at[it, s, way], edge_r.at[it, s, way], where,
                )
                copy.start()
                copies.append(copy)
            for start in range(W, grown - W, W):
                sum_columns(terms, s, start)
            return copies

        def add_edges(s, copies):
            for copy in copies:
                copy.wait_recv()
            rows = pl.ds(2 * s, 2)
            acc[rows, :, pl.ds(0, W)] = acc[rows, :, pl.ds(0, W)] + edge_recv[it, 0, s].astype(F32)
            acc[rows, :, pl.ds(grown - W, W)] = acc[rows, :, pl.ds(grown - W, W)] + edge_recv[it, 1, s].astype(F32)

        def squares(s):
            inner = acc[pl.ds(2 * s, 2), :, pl.ds(M, block_cols)].reshape(2 * M // 8, 8, block_cols)
            summed = jnp.sum(inner * inner, axis=0)
            total = summed[:, :M]
            for i in range(1, block_cols // M):
                total = total + summed[:, i * M : (i + 1) * M]
            return total

        for copy in halo[0]:
            copy.wait_recv()
        for k in range(MOST):
            for c in range(2):
                found = window(it, 0, k, c)
                patch[k, c] = found if it == 0 else patch[k, c] - scale * found
            re = probe[0] * patch[k, 0] - probe[1] * patch[k, 1]
            im = probe[0] * patch[k, 1] + probe[1] * patch[k, 0]
            put(k, re, im)
        for k in range(MOST):
            a, b = transform(k, 0)
            put(k, spread[0] * a - spread[1] * b, spread[0] * b + spread[1] * a)
        for copy in halo[1]:
            copy.wait_recv()
        for k in range(MOST):
            for c in range(2):
                found = window(it, 1, k, c)
                patch[k, 2 + c] = found if it == 0 else patch[k, 2 + c] - scale * found
        if it > 0:
            fld[...] = fld[...] - scale * acc[:, :, pl.ds(M, block_cols)]
        for k in range(MOST):
            a, b = transform(k, 1)
            psi1[k, 0] = a
            psi1[k, 1] = b
            put(k, a * patch[k, 2] - b * patch[k, 3], a * patch[k, 3] + b * patch[k, 2])
        for k in range(MOST):
            a, b = transform(k, 0)
            misfit = jnp.where(mine[k][3] > 0, a * a + b * b - wanted[k], 0.0)
            put(k, misfit * a, misfit * b)

        for k in range(MOST):
            a, b = transform(k, 1)
            put(k, patch[k, 2] * a + patch[k, 3] * b, patch[k, 2] * b - patch[k, 3] * a)
            fold_out(k, 1, 0, psi1[k, 0] * a + psi1[k, 1] * b)
            fold_out(k, 1, 1, psi1[k, 0] * b - psi1[k, 1] * a)
        fold1 = start_fold(1)
        for k in range(MOST):
            a, b = transform(k, 0)
            put(k, spread[0] * a + spread[1] * b, spread[0] * b - spread[1] * a)
        for k in range(MOST):
            a, b = transform(k, 1)
            fold_out(k, 0, 0, probe[0] * a + probe[1] * b)
            fold_out(k, 0, 1, probe[0] * b - probe[1] * a)
            re = patch[k, 0] * a + patch[k, 1] * b
            im = patch[k, 0] * b - patch[k, 1] * a
            if k == 0:
                pg[pl.ds(0, W)] = re
                pg[pl.ds(W, W)] = im
            else:
                pg[pl.ds(0, W)] = pg[pl.ds(0, W)] + re
                pg[pl.ds(W, W)] = pg[pl.ds(W, W)] + im
        fold0 = start_fold(0)

        rs1_send[it] = pg[...].astype(BF16).reshape(ng, chunk, W)
        for j in range(1, ng):
            remote(
                rs1_send.at[it, g_index(j)], rs1.at[it, me_g], p_s.at[it, 0], p_r.at[it, 0], g_peer(j)
            ).start()
        rs1[it, me_g] = rs1_send[it, me_g]

        for copy in fold1:
            copy.wait_recv()
        edge1 = sum_slice(1)
        for copy in fold0:
            copy.wait_recv()
        edge0 = sum_slice(0)

        wait_bytes(rs1.at[it, pl.ds(0, ng - 1)], p_r.at[it, 0])
        rs2_send[it] = jnp.sum(rs1[it].astype(F32), axis=0).astype(BF16)
        for j in range(1, nw):
            remote(rs2_send.at[it], rs2.at[it, wi], p_s.at[it, 1], p_r.at[it, 1], w_peer(j)).start()
        rs2[it, wi] = rs2_send[it]

        more = it + 1 < ITERS
        sends += fold0 + fold1 + edge0 + edge1 + halo[0] + halo[1]
        halo = [None, None]
        for s, copies in ((1, edge1), (0, edge0)):
            add_edges(s, copies)
            if more:
                steps[pl.ds(2 * s, 2)] = acc[pl.ds(2 * s, 2)].astype(BF16)
                halo[s] = start_halo(it + 1, s, steps)
        sq_sa[it] = squares(0) + squares(1)
        for j in range(1, ng):
            remote(sq_sa.at[it], sq_a.at[it, me_g], q_s.at[it, 0], q_r.at[it, 0], g_peer(j)).start()
        sq_a[it, me_g] = sq_sa[it]

        wait_bytes(rs2.at[it, pl.ds(0, nw - 1)], p_r.at[it, 1])
        ag_send[it] = jnp.sum(rs2[it].astype(F32), axis=0).astype(BF16)
        for j in range(1, ng):
            remote(ag_send.at[it], ag.at[it, me_g], p_s.at[it, 2], p_r.at[it, 2], g_peer(j)).start()
        ag[it, me_g] = ag_send[it]

        if more:
            for s in range(2):
                own_columns(it + 1, s, steps)

        wait_bytes(sq_a.at[it, pl.ds(0, ng - 1)], q_r.at[it, 0])
        sq_sb[it] = jnp.sum(sq_a[it], axis=0)
        for j in range(1, nw):
            remote(sq_sb.at[it], sq_b.at[it, wi], q_s.at[it, 1], q_r.at[it, 1], w_peer(j)).start()
        sq_b[it, wi] = sq_sb[it]

        wait_bytes(ag.at[it, pl.ds(0, ng - 1)], p_r.at[it, 2])
        grad = ag[it].astype(F32).reshape(2, W, W)
        mean = jnp.sum(grad * grad) / float(2 * W * W)
        probe[...] = probe[...] - ETA_PROBE * lax.rsqrt(mean + 1e-06) * grad

        wait_bytes(sq_b.at[it, pl.ds(0, nw - 1)], q_r.at[it, 1])
        mean = jnp.sum(jnp.sum(sq_b[it], axis=0)) / cells
        scale = ETA_OBJECT * lax.rsqrt(mean + 1e-06)

    stores = [pltpu.make_async_copy(probe, probe_out, local_sem.at[4])]
    stores[0].start()
    for c in range(4):
        fld[c] = fld[c] - scale * acc[c, :, pl.ds(M, block_cols)]
        store = pltpu.make_async_copy(fld.at[c], obj_out.at[c], local_sem.at[c])
        store.start()
        stores.append(store)
    for copy in sends:
        copy.wait_send()
    for it in range(ITERS):
        wait_bytes(rs1_send.at[it, pl.ds(0, ng - 1)], p_s.at[it, 0])
        wait_bytes(rs2.at[it, pl.ds(0, nw - 1)], p_s.at[it, 1])
        wait_bytes(ag.at[it, pl.ds(0, ng - 1)], p_s.at[it, 2])
        wait_bytes(sq_a.at[it, pl.ds(0, ng - 1)], q_s.at[it, 0])
        wait_bytes(sq_b.at[it, pl.ds(0, nw - 1)], q_s.at[it, 1])
    for store in stores:
        store.wait()


def per_device(object_slices, probe, patterns, offsets, owner):
    nslice, _, rows, cols = object_slices.shape
    bands = patterns.shape[0]
    npos, ntile = lax.axis_size("pos"), lax.axis_size("tile")
    nw = 8 if npos % 8 == 0 else 2
    ng = npos // nw * ntile
    chunk = 2 * W // ng
    grown = cols + 2 * M
    cells = float(nslice * 2 * rows * cols * npos * ntile)
    dft, spread = tables()
    vmem, dma = pltpu.VMEM, pltpu.SemaphoreType.DMA
    any_space = pl.BlockSpec(memory_space=pl.ANY)
    scratch = [
        pltpu.SMEM((bands, 2), jnp.int32),
        pltpu.SMEM((bands,), jnp.int32),
        pltpu.SMEM((2, bands, 2), jnp.int32),
        pltpu.SMEM((2, bands), jnp.int32),
        vmem((4, M, cols), F32),
        vmem((4, M, grown), F32),
        vmem((4, M, grown), BF16),
        vmem((4, M, grown), BF16),
        vmem((ITERS, 3, 2, MOST, 2, M, W), BF16),
        vmem((ITERS, 2, 2, MOST, 2, M, W), BF16),
        vmem((ITERS, 2, 2, MOST, 2, M, W), BF16),
        vmem((ITERS, 3, 2, MOST, 2, M, W), BF16),
        vmem((ITERS, 2, 2, 2, M, W), BF16),
        vmem((ITERS, 2, 2, 2, M, W), BF16),
        vmem((2, W, W), F32),
        vmem((bands, W, W), F32),
        vmem((MOST, W, W), F32),
        vmem((2, 2 * W, 2 * W), BF16),
        vmem((2, W, W), F32),
        vmem((3 * MOST * W, grown), BF16),
        vmem((MOST, W, 3 * M), BF16),
        vmem((MOST, 3 * M, W), BF16),
        vmem((MOST, 4, W, W), F32),
        vmem((MOST, W, 2 * W), BF16),
        vmem((MOST, 2 * W, W), BF16),
        vmem((MOST, 2, W, W), F32),
        vmem((2 * W, W), F32),
        vmem((ITERS, ng, chunk, W), BF16),
        vmem((ITERS, ng, chunk, W), BF16),
        vmem((ITERS, chunk, W), BF16),
        vmem((ITERS, nw, chunk, W), BF16),
        vmem((ITERS, chunk, W), BF16),
        vmem((ITERS, ng, chunk, W), BF16),
        vmem((ITERS, ng, 8, M), F32),
        vmem((ITERS, nw, 8, M), F32),
        vmem((ITERS, 8, M), F32),
        vmem((ITERS, 8, M), F32),
        dma((7,)),
        dma((4,)), dma((4,)),
        dma((2, 2)), dma((2, 2)),
        dma((ITERS, 2, 2)), dma((ITERS, 2, 2)),
        dma((ITERS, 2, 2)), dma((ITERS, 2, 2)),
        dma((ITERS, 2, 2)), dma((ITERS, 2, 2)),
        dma((ITERS, 3)), dma((ITERS, 3)),
        dma((ITERS, 2)), dma((ITERS, 2)),
    ]
    field, current = pl.pallas_call(
        functools.partial(body, (npos, ntile, nw, bands, cols, cells)),
        out_shape=(
            jax.ShapeDtypeStruct((4, rows, cols), F32),
            jax.ShapeDtypeStruct((2, W, W), F32),
        ),
        in_specs=[any_space] * 7,
        out_specs=(any_space, any_space),
        scratch_shapes=scratch,
        compiler_params=pltpu.CompilerParams(
            collective_id=0, has_side_effects=True, vmem_limit_bytes=48 * 1024 * 1024
        ),
    )(
        offsets,
        owner,
        object_slices.reshape(4, rows, cols),
        probe,
        patterns,
        jnp.asarray(dft),
        jnp.asarray(spread),
    )
    return field.reshape(nslice, 2, rows, cols), current


def solution(mesh):
    return jax.shard_map(
        per_device,
        mesh=mesh,
        in_specs=(
            P(None, None, "pos", "tile"),
            P(),
            P("pos", None, None),
            P("pos", None),
            P("pos"),
        ),
        out_specs=(P(None, None, "pos", "tile"), P()),
        check_vma=False,
    )
```

```python
import functools
import math

import jax
import jax.numpy as jnp
import numpy as np
from jax import lax
from jax.experimental import pallas as pl
from jax.experimental.pallas import tpu as pltpu
from jax.sharding import PartitionSpec as P

ITERS = 2
MOST = 2
FRESNEL = 0.05
ETA_OBJECT = 0.5
ETA_PROBE = 0.5
W = 256
M = 128
MESH = pl.DeviceIdType.MESH
F32 = jnp.float32
BF16 = jnp.bfloat16


def tables():
    indices = np.arange(W)
    angles = (indices[:, None] * indices[None, :] % W) * (2.0 * math.pi / W)
    cosine = np.cos(angles) / math.sqrt(W)
    sine = np.sin(angles) / math.sqrt(W)
    ahead = np.block([[cosine, -sine], [sine, cosine]])
    behind = np.block([[cosine, sine], [-sine, cosine]])
    dft = np.stack([ahead, behind]).astype(np.float32).astype(jnp.bfloat16)
    frequency = ((indices + W // 2) % W - W // 2).astype(np.float32)
    phases = -math.pi * FRESNEL / W * (frequency[:, None] ** 2 + frequency[None, :] ** 2)
    spread = np.stack([np.cos(phases), np.sin(phases)]).astype(np.float32)
    return dft, spread


def slot_info(owner_of, offset_of, bands, tile):
    zero = jnp.int32(0)
    found = zero
    slots = [[zero, zero, zero, zero] for _ in range(MOST)]
    for n in range(bands):
        live = owner_of(n) == tile
        row, col = offset_of(n, 0) + M, offset_of(n, 1) + M
        for k in range(MOST):
            here = jnp.logical_and(live, found == k)
            slots[k] = [
                jnp.where(here, new, old)
                for new, old in zip((row, col, jnp.int32(n), jnp.int32(1)), slots[k])
            ]
        found = found + live.astype(jnp.int32)
    return slots


def one_hot(rows, cols, shift):
    row = lax.broadcasted_iota(jnp.int32, (rows, cols), 0)
    col = lax.broadcasted_iota(jnp.int32, (rows, cols), 1)
    return (row == col + shift).astype(F32).astype(BF16)


def dot(a, b):
    return jnp.dot(a, b, preferred_element_type=F32)


def body(sizes, *refs):
    (npos, ntile, nw, bands, block_cols, cells) = sizes
    (off_in, own_in, obj, probe_in, pats_in, tab_in, spread_in, obj_out, probe_out) = refs[:9]
    (
        off, own, off_nb, own_nb, fld, acc, low0, low1, steps, parts, halo_send, fold_send, contrib, edge_send, edge_recv,
        probe, pats, wanted, tab, spread, sel, place, rows_in, rows_out, patch, x, mid, psi1, pg,
        rs1_send, rs1, rs2_send, rs2, ag_send, ag, sq_a, sq_b, sq_sa, sq_sb,
        local_sem, info_s, info_r, col_s, col_r, halo_s, halo_r, fold_s, fold_r, edge_s, edge_r,
        p_s, p_r, q_s, q_r,
    ) = refs[9:]
    inner = block_cols // M
    low = (low0, low1)
    ntiles = inner + 2
    nx = npos // nw
    ng = nx * ntile
    chunk = 2 * W // ng
    p = lax.axis_index("pos")
    t = lax.axis_index("tile")
    xi, wi = p // nw, p % nw
    me_g = xi * ntile + t

    up = {"pos": lax.rem(p + npos - 1, npos)}
    down = {"pos": lax.rem(p + 1, npos)}
    left = {"tile": lax.rem(t + ntile - 1, ntile)}
    right = {"tile": lax.rem(t + 1, ntile)}

    def g_peer(j):
        return {
            "pos": lax.rem(xi + j // ntile, nx) * nw + wi,
            "tile": lax.rem(t + j % ntile, ntile),
        }

    def g_index(j):
        return lax.rem(xi + j // ntile, nx) * ntile + lax.rem(t + j % ntile, ntile)

    def w_peer(j):
        return {"pos": xi * nw + lax.rem(wi + j, nw)}

    def remote(src, dst, send, recv, where):
        return pltpu.make_async_remote_copy(
            src_ref=src, dst_ref=dst, send_sem=send, recv_sem=recv, device_id=where, device_id_type=MESH
        )

    def wait_bytes(ref, sem):
        pltpu.make_async_copy(ref, ref, sem).wait()

    loads = [
        pltpu.make_async_copy(off_in, off, local_sem.at[0]),
        pltpu.make_async_copy(own_in, own, local_sem.at[1]),
        pltpu.make_async_copy(obj, fld, local_sem.at[2]),
        pltpu.make_async_copy(pats_in, pats, local_sem.at[3]),
        pltpu.make_async_copy(probe_in, probe, local_sem.at[4]),
        pltpu.make_async_copy(tab_in, tab, local_sem.at[5]),
        pltpu.make_async_copy(spread_in, spread, local_sem.at[6]),
    ]
    for load in loads:
        load.start()

    barrier = pltpu.get_barrier_semaphore()
    friends = [up, down, left, right]
    friends += [g_peer(j) for j in range(1, ng)]
    friends += [w_peer(j) for j in range(1, nw)]
    for friend in friends:
        pl.semaphore_signal(barrier, inc=1, device_id=friend, device_id_type=MESH)
    for load in loads[:3]:
        load.wait()
    for s in range(2):
        for j in range(inner):
            low[s][1 + j] = fld[pl.ds(2 * s, 2), :, pl.ds(j * M, M)].reshape(2 * M, M).astype(BF16)
    pl.semaphore_wait(barrier, len(friends))

    info = [
        remote(off, off_nb.at[0], info_s.at[0], info_r.at[0], down),
        remote(own, own_nb.at[0], info_s.at[1], info_r.at[1], down),
        remote(off, off_nb.at[1], info_s.at[2], info_r.at[2], up),
        remote(own, own_nb.at[1], info_s.at[3], info_r.at[3], up),
    ]
    for copy in info:
        copy.start()
    cols = []
    for s in range(2):
        cols.append([
            remote(low[s].at[inner], low[s].at[0], col_s.at[s, 0], col_r.at[s, 0], right),
            remote(low[s].at[1], low[s].at[inner + 1], col_s.at[s, 1], col_r.at[s, 1], left),
        ])
        for copy in cols[s]:
            copy.start()
    sends = info + cols[0] + cols[1]

    firsts = [None] * (3 * MOST)

    def build_sel(k, slot):
        firsts[k] = jnp.minimum(slot[1] // M, inner - 1)
        sel[k] = one_hot(3 * M, W, slot[1] - firsts[k] * M)

    mine = slot_info(lambda n: own[n], lambda n, i: off[i, n], bands, t)
    for k in range(MOST):
        build_sel(MOST + k, mine[k])
        rows_in[k] = (
            lax.broadcasted_iota(jnp.int32, (W, 3 * M), 1)
            == lax.broadcasted_iota(jnp.int32, (W, 3 * M), 0) + mine[k][0]
        ).astype(F32).astype(BF16)
        rows_out[k] = one_hot(3 * M, W, mine[k][0])
    for copy in info:
        copy.wait_recv()
    above = slot_info(lambda n: own_nb[0, n], lambda n, i: off_nb[0, i, n], bands, t)
    below = slot_info(lambda n: own_nb[1, n], lambda n, i: off_nb[1, i, n], bands, t)
    for k in range(MOST):
        build_sel(k, above[k])
        build_sel(2 * MOST + k, below[k])

    def chosen(source, k):
        first = firsts[k]
        near = jnp.concatenate([source[first], source[first + 1], source[first + 2]], axis=1)
        return dot(near, sel[k]).astype(BF16).reshape(2, M, W)

    def start_halo(h, s, source):
        copies = []
        for way, (group, part, where) in enumerate(((0, 2, up), (2, 0, down))):
            for k in range(MOST):
                halo_send[h, way, s, k] = chosen(source, group * MOST + k)
            copy = remote(
                halo_send.at[h, way, s], parts.at[h, part, s], halo_s.at[h, s, way], halo_r.at[h, s, way], where
            )
            copy.start()
            copies.append(copy)
        return copies

    def own_columns(h, s, source):
        for k in range(MOST):
            parts[h, 1, s, k] = chosen(source, MOST + k)

    def window(h, s, k, c):
        stack = jnp.concatenate([parts[h, 0, s, k, c], parts[h, 1, s, k, c], parts[h, 2, s, k, c]], axis=0)
        return dot(rows_in[k], stack)

    halo = []
    for s in range(2):
        for copy in cols[s]:
            copy.wait_recv()
        halo.append(start_halo(0, s, low[s]))
    for s in range(2):
        own_columns(0, s, low[s])
    for load in loads[3:]:
        load.wait()
    for k in range(MOST):
        found = pats[0]
        for n in range(1, bands):
            found = jnp.where(mine[k][2] == n, pats[n], found)
        wanted[k] = found
    for k, slot in enumerate(above + mine + below):
        place[pl.ds(k * W, W), :] = (
            lax.broadcasted_iota(jnp.int32, (W, ntiles * M), 1)
            == lax.broadcasted_iota(jnp.int32, (W, ntiles * M), 0) + slot[1]
        ).astype(F32).astype(BF16)

    def transform(k, way):
        half = dot(x[k], tab[way]).astype(BF16)
        mid[k, pl.ds(0, W)] = half[:, :W]
        mid[k, pl.ds(W, W)] = half[:, W:]
        both = dot(tab[1 - way], mid[k])
        return both[:W], both[W:]

    def put(k, re, im):
        x[k, :, pl.ds(0, W)] = re.astype(BF16)
        x[k, :, pl.ds(W, W)] = im.astype(BF16)

    for it in range(ITERS):

        def fold_out(k, s, c, value):
            rows = dot(rows_out[k], value.astype(BF16)).astype(BF16)
            fold_send[it, 0, s, k, c] = rows[:M]
            contrib[it, 1, s, k, c] = rows[M : 2 * M]
            fold_send[it, 1, s, k, c] = rows[2 * M :]

        def start_fold(s):
            copies = [
                remote(
                    fold_send.at[it, 0, s], contrib.at[it, 2, s], fold_s.at[it, s, 0], fold_r.at[it, s, 0], up
                ),
                remote(
                    fold_send.at[it, 1, s], contrib.at[it, 0, s], fold_s.at[it, s, 1], fold_r.at[it, s, 1], down
                ),
            ]
            for copy in copies:
                copy.start()
            return copies

        def sum_columns(terms, s, j):
            both = dot(terms, place[:, pl.ds(j * M, 2 * M)])
            acc[s, j] = both[:, :M]
            acc[s, j + 1] = both[:, M:]

        def sum_edges(s):
            terms = jnp.concatenate(
                [contrib[it, g, s, k].reshape(2 * M, W) for g in range(3) for k in range(MOST)], axis=1
            )
            copies = []
            for way, (j, where) in enumerate(((0, left), (ntiles - 2, right))):
                sum_columns(terms, s, j)
                edge_send[it, way, s] = acc[s, pl.ds(j, 2)].astype(BF16)
                copy = remote(
                    edge_send.at[it, way, s], edge_recv.at[it, 1 - way, s],
                    edge_s.at[it, s, way], edge_r.at[it, s, way], where,
                )
                copy.start()
                copies.append(copy)
            return terms, copies

        def add_edges(s, copies):
            for copy in copies:
                copy.wait_recv()
            acc[s, pl.ds(0, 2)] = acc[s, pl.ds(0, 2)] + edge_recv[it, 0, s].astype(F32)
            acc[s, pl.ds(ntiles - 2, 2)] = acc[s, pl.ds(ntiles - 2, 2)] + edge_recv[it, 1, s].astype(F32)

        def squares(s, j, count):
            values = acc[s, pl.ds(j, count)].reshape(count * 2 * M // 8, 8, M)
            return jnp.sum(values * values, axis=0)

        for copy in halo[0]:
            copy.wait_recv()
        for k in range(MOST):
            for c in range(2):
                found = window(it, 0, k, c)
                patch[k, c] = found if it == 0 else patch[k, c] - scale * found
            re = probe[0] * patch[k, 0] - probe[1] * patch[k, 1]
            im = probe[0] * patch[k, 1] + probe[1] * patch[k, 0]
            put(k, re, im)
        for k in range(MOST):
            a, b = transform(k, 0)
            put(k, spread[0] * a - spread[1] * b, spread[0] * b + spread[1] * a)
        for copy in halo[1]:
            copy.wait_recv()
        for k in range(MOST):
            for c in range(2):
                found = window(it, 1, k, c)
                patch[k, 2 + c] = found if it == 0 else patch[k, 2 + c] - scale * found
        if it > 0:
            for s in range(2):
                for j in range(inner):
                    here = (pl.ds(2 * s, 2), slice(None), pl.ds(j * M, M))
                    fld[here] = fld[here] - scale * acc[s, 1 + j].reshape(2, M, M)
        for k in range(MOST):
            a, b = transform(k, 1)
            psi1[k, 0] = a
            psi1[k, 1] = b
            put(k, a * patch[k, 2] - b * patch[k, 3], a * patch[k, 3] + b * patch[k, 2])
        for k in range(MOST):
            a, b = transform(k, 0)
            misfit = jnp.where(mine[k][3] > 0, a * a + b * b - wanted[k], 0.0)
            put(k, misfit * a, misfit * b)

        for k in range(MOST):
            a, b = transform(k, 1)
            put(k, patch[k, 2] * a + patch[k, 3] * b, patch[k, 2] * b - patch[k, 3] * a)
            fold_out(k, 1, 0, psi1[k, 0] * a + psi1[k, 1] * b)
            fold_out(k, 1, 1, psi1[k, 0] * b - psi1[k, 1] * a)
        fold1 = start_fold(1)
        for k in range(MOST):
            a, b = transform(k, 0)
            put(k, spread[0] * a + spread[1] * b, spread[0] * b - spread[1] * a)
        for k in range(MOST):
            a, b = transform(k, 1)
            fold_out(k, 0, 0, probe[0] * a + probe[1] * b)
            fold_out(k, 0, 1, probe[0] * b - probe[1] * a)
            re = patch[k, 0] * a + patch[k, 1] * b
            im = patch[k, 0] * b - patch[k, 1] * a
            if k == 0:
                pg[pl.ds(0, W)] = re
                pg[pl.ds(W, W)] = im
            else:
                pg[pl.ds(0, W)] = pg[pl.ds(0, W)] + re
                pg[pl.ds(W, W)] = pg[pl.ds(W, W)] + im
        fold0 = start_fold(0)

        rs1_send[it] = pg[...].astype(BF16).reshape(ng, chunk, W)
        for j in range(1, ng):
            remote(
                rs1_send.at[it, g_index(j)], rs1.at[it, me_g], p_s.at[it, 0], p_r.at[it, 0], g_peer(j)
            ).start()
        rs1[it, me_g] = rs1_send[it, me_g]

        for copy in fold1:
            copy.wait_recv()
        terms, edge1 = sum_edges(1)
        for j in range(2, ntiles - 2, 2):
            sum_columns(terms, 1, j)
        for copy in fold0:
            copy.wait_recv()
        terms, edge0 = sum_edges(0)

        wait_bytes(rs1.at[it, pl.ds(0, ng - 1)], p_r.at[it, 0])
        rs2_send[it] = jnp.sum(rs1[it].astype(F32), axis=0).astype(BF16)
        for j in range(1, nw):
            remote(rs2_send.at[it], rs2.at[it, wi], p_s.at[it, 1], p_r.at[it, 1], w_peer(j)).start()
        rs2[it, wi] = rs2_send[it]

        more = it + 1 < ITERS
        sends += fold0 + fold1 + edge0 + edge1 + halo[0] + halo[1]
        halo = [None, None]
        add_edges(1, edge1)
        if more:
            steps[1] = acc[1].astype(BF16)
            halo[1] = start_halo(it + 1, 1, steps.at[1])
        for j in range(2, ntiles - 2, 2):
            sum_columns(terms, 0, j)
        total = squares(1, 1, inner) + squares(0, 2, inner - 2)
        add_edges(0, edge0)
        if more:
            steps[0] = acc[0].astype(BF16)
            halo[0] = start_halo(it + 1, 0, steps.at[0])
        sq_sa[it] = total + squares(0, 1, 1) + squares(0, inner, 1)
        for j in range(1, ng):
            remote(sq_sa.at[it], sq_a.at[it, me_g], q_s.at[it, 0], q_r.at[it, 0], g_peer(j)).start()
        sq_a[it, me_g] = sq_sa[it]

        wait_bytes(rs2.at[it, pl.ds(0, nw - 1)], p_r.at[it, 1])
        ag_send[it] = jnp.sum(rs2[it].astype(F32), axis=0).astype(BF16)
        for j in range(1, ng):
            remote(ag_send.at[it], ag.at[it, me_g], p_s.at[it, 2], p_r.at[it, 2], g_peer(j)).start()
        ag[it, me_g] = ag_send[it]

        wait_bytes(sq_a.at[it, pl.ds(0, ng - 1)], q_r.at[it, 0])
        sq_sb[it] = jnp.sum(sq_a[it], axis=0)
        for j in range(1, nw):
            remote(sq_sb.at[it], sq_b.at[it, wi], q_s.at[it, 1], q_r.at[it, 1], w_peer(j)).start()
        sq_b[it, wi] = sq_sb[it]
        if more:
            for s in range(2):
                own_columns(it + 1, s, steps.at[s])

        wait_bytes(ag.at[it, pl.ds(0, ng - 1)], p_r.at[it, 2])
        grad = ag[it].astype(F32).reshape(2, W, W)
        mean = jnp.sum(grad * grad) / float(2 * W * W)
        probe[...] = probe[...] - ETA_PROBE * lax.rsqrt(mean + 1e-06) * grad

        wait_bytes(sq_b.at[it, pl.ds(0, nw - 1)], q_r.at[it, 1])
        mean = jnp.sum(jnp.sum(sq_b[it], axis=0)) / cells
        scale = ETA_OBJECT * lax.rsqrt(mean + 1e-06)

    for s in range(2):
        for j in range(inner):
            here = (pl.ds(2 * s, 2), slice(None), pl.ds(j * M, M))
            obj_out[here] = fld[here] - scale * acc[s, 1 + j].reshape(2, M, M)
    probe_out[...] = probe[...]
    for copy in sends:
        copy.wait_send()
    for it in range(ITERS):
        wait_bytes(rs1_send.at[it, pl.ds(0, ng - 1)], p_s.at[it, 0])
        wait_bytes(rs2.at[it, pl.ds(0, nw - 1)], p_s.at[it, 1])
        wait_bytes(ag.at[it, pl.ds(0, ng - 1)], p_s.at[it, 2])
        wait_bytes(sq_a.at[it, pl.ds(0, ng - 1)], q_s.at[it, 0])
        wait_bytes(sq_b.at[it, pl.ds(0, nw - 1)], q_s.at[it, 1])


def per_device(object_slices, probe, patterns, offsets, owner):
    nslice, _, rows, cols = object_slices.shape
    bands = patterns.shape[0]
    npos, ntile = lax.axis_size("pos"), lax.axis_size("tile")
    nw = 8 if npos % 8 == 0 else 2
    ng = npos // nw * ntile
    chunk = 2 * W // ng
    ntiles = cols // M + 2
    cells = float(nslice * 2 * rows * cols * npos * ntile)
    dft, spread = tables()
    vmem, dma = pltpu.VMEM, pltpu.SemaphoreType.DMA
    any_space = pl.BlockSpec(memory_space=pl.ANY)
    scratch = [
        pltpu.SMEM((2, bands), jnp.int32),
        pltpu.SMEM((bands,), jnp.int32),
        pltpu.SMEM((2, 2, bands), jnp.int32),
        pltpu.SMEM((2, bands), jnp.int32),
        vmem((4, M, cols), F32),
        vmem((2, ntiles, 2 * M, M), F32),
        vmem((ntiles, 2 * M, M), BF16),
        vmem((ntiles, 2 * M, M), BF16),
        vmem((2, ntiles, 2 * M, M), BF16),
        vmem((ITERS, 3, 2, MOST, 2, M, W), BF16),
        vmem((ITERS, 2, 2, MOST, 2, M, W), BF16),
        vmem((ITERS, 2, 2, MOST, 2, M, W), BF16),
        vmem((ITERS, 3, 2, MOST, 2, M, W), BF16),
        vmem((ITERS, 2, 2, 2, 2 * M, M), BF16),
        vmem((ITERS, 2, 2, 2, 2 * M, M), BF16),
        vmem((2, W, W), F32),
        vmem((bands, W, W), F32),
        vmem((MOST, W, W), F32),
        vmem((2, 2 * W, 2 * W), BF16),
        vmem((2, W, W), F32),
        vmem((3 * MOST, 3 * M, W), BF16),
        vmem((3 * MOST * W, ntiles * M), BF16),
        vmem((MOST, W, 3 * M), BF16),
        vmem((MOST, 3 * M, W), BF16),
        vmem((MOST, 4, W, W), F32),
        vmem((MOST, W, 2 * W), BF16),
        vmem((MOST, 2 * W, W), BF16),
        vmem((MOST, 2, W, W), F32),
        vmem((2 * W, W), F32),
        vmem((ITERS, ng, chunk, W), BF16),
        vmem((ITERS, ng, chunk, W), BF16),
        vmem((ITERS, chunk, W), BF16),
        vmem((ITERS, nw, chunk, W), BF16),
        vmem((ITERS, chunk, W), BF16),
        vmem((ITERS, ng, chunk, W), BF16),
        vmem((ITERS, ng, 8, M), F32),
        vmem((ITERS, nw, 8, M), F32),
        vmem((ITERS, 8, M), F32),
        vmem((ITERS, 8, M), F32),
        dma((7,)),
        dma((4,)), dma((4,)),
        dma((2, 2)), dma((2, 2)),
        dma((ITERS, 2, 2)), dma((ITERS, 2, 2)),
        dma((ITERS, 2, 2)), dma((ITERS, 2, 2)),
        dma((ITERS, 2, 2)), dma((ITERS, 2, 2)),
        dma((ITERS, 3)), dma((ITERS, 3)),
        dma((ITERS, 2)), dma((ITERS, 2)),
    ]
    operands = (
        offsets.T,
        owner,
        object_slices.reshape(4, rows, cols),
        probe,
        patterns,
        jnp.asarray(dft),
        jnp.asarray(spread),
    )
    field, current = pl.pallas_call(
        functools.partial(body, (npos, ntile, nw, bands, cols, cells)),
        out_shape=(pltpu.VMEM((4, rows, cols), F32), pltpu.VMEM((2, W, W), F32)),
        in_specs=[any_space] * 7,
        out_specs=(pl.BlockSpec(memory_space=pltpu.VMEM),) * 2,
        scratch_shapes=scratch,
        compiler_params=pltpu.CompilerParams(
            collective_id=0, has_side_effects=True, vmem_limit_bytes=48 * 1024 * 1024
        ),
    )(*(pltpu.with_memory_space_constraint(operand, pltpu.HBM) for operand in operands))
    return field.reshape(nslice, 2, rows, cols), current


def solution(mesh):
    return jax.shard_map(
        per_device,
        mesh=mesh,
        in_specs=(
            P(None, None, "pos", "tile"),
            P(),
            P("pos", None, None),
            P("pos", None),
            P("pos"),
        ),
        out_specs=(P(None, None, "pos", "tile"), P()),
        check_vma=False,
    )
```

```python
import functools
import math

import jax
import jax.numpy as jnp
import numpy as np
from jax import lax
from jax.experimental import pallas as pl
from jax.experimental.pallas import tpu as pltpu
from jax.sharding import PartitionSpec as P

ITERS = 2
MOST = 2
FRESNEL = 0.05
ETA_OBJECT = 0.5
ETA_PROBE = 0.5
W = 256
M = 128
MESH = pl.DeviceIdType.MESH
F32 = jnp.float32
BF16 = jnp.bfloat16


def tables():
    indices = np.arange(W)
    angles = (indices[:, None] * indices[None, :] % W) * (2.0 * math.pi / W)
    cosine = np.cos(angles) / math.sqrt(W)
    sine = np.sin(angles) / math.sqrt(W)
    ahead = np.block([[cosine, -sine], [sine, cosine]])
    behind = np.block([[cosine, sine], [-sine, cosine]])
    dft = np.stack([ahead, behind]).astype(np.float32).astype(jnp.bfloat16)
    frequency = ((indices + W // 2) % W - W // 2).astype(np.float32)
    phases = -math.pi * FRESNEL / W * (frequency[:, None] ** 2 + frequency[None, :] ** 2)
    spread = np.stack([np.cos(phases), np.sin(phases)]).astype(np.float32)
    return dft, spread


def slot_info(owner_of, offset_of, bands, tile):
    zero = jnp.int32(0)
    found = zero
    slots = [[zero, zero, zero, zero] for _ in range(MOST)]
    for n in range(bands):
        live = owner_of(n) == tile
        row, col = offset_of(n, 0) + M, offset_of(n, 1) + M
        for k in range(MOST):
            here = jnp.logical_and(live, found == k)
            slots[k] = [
                jnp.where(here, new, old)
                for new, old in zip((row, col, jnp.int32(n), jnp.int32(1)), slots[k])
            ]
        found = found + live.astype(jnp.int32)
    return slots


def one_hot(rows, cols, shift):
    row = lax.broadcasted_iota(jnp.int32, (rows, cols), 0)
    col = lax.broadcasted_iota(jnp.int32, (rows, cols), 1)
    return (row == col + shift).astype(F32).astype(BF16)


def dot(a, b):
    return jnp.dot(a, b, preferred_element_type=F32)


def body(sizes, *refs):
    (npos, ntile, nw, bands, block_cols, cells) = sizes
    (off_in, own_in, obj, probe_in, pats_in, tab_in, spread_in, obj_out, probe_out) = refs[:9]
    (
        off, own, off_nb, own_nb, fld, acc, low0, low1, steps, parts, halo_send, fold_send, contrib, edge_send, edge_recv,
        probe, pats, wanted, tab, spread, sel, place, rows_in, rows_out, patch, x, mid, psi1, pg,
        pair_send, pair, rs1_send, rs1, rs2_send, rs2, ag, sq_all, sq_send,
        local_sem, info_s, info_r, col_s, col_r, halo_s, halo_r, fold_s, fold_r, edge_s, edge_r,
        p_s, p_r, q_s, q_r, pair_s, pair_r,
    ) = refs[9:]
    inner = block_cols // M
    low = (low0, low1)
    ntiles = inner + 2
    nx = npos // nw
    ng = nx * ntile
    nz = nw // 2
    p = lax.axis_index("pos")
    t = lax.axis_index("tile")
    xi, wi = p // nw, p % nw
    zi, ci = wi // 2, wi % 2
    me_g = xi * ntile + t
    chips = npos // 2 * ntile
    me = p // 2 * ntile + t

    up = {"pos": lax.rem(p + npos - 1, npos)}
    down = {"pos": lax.rem(p + 1, npos)}
    left = {"tile": lax.rem(t + ntile - 1, ntile)}
    right = {"tile": lax.rem(t + 1, ntile)}

    def g_peer(j):
        return {
            "pos": lax.rem(xi + j // ntile, nx) * nw + wi,
            "tile": lax.rem(t + j % ntile, ntile),
        }

    def g_index(j):
        return lax.rem(xi + j // ntile, nx) * ntile + lax.rem(t + j % ntile, ntile)

    def w_peer(j):
        return {"pos": xi * nw + lax.rem(wi + j, nw)}

    def z_peer(j):
        return {"pos": xi * nw + lax.rem(zi + j, nz) * 2 + ci}

    twin = {"pos": xi * nw + zi * 2 + 1 - ci}

    def chip_peer(j):
        return {"pos": lax.rem(p + j // ntile * 2, npos), "tile": lax.rem(t + j % ntile, ntile)}

    def remote(src, dst, send, recv, where):
        return pltpu.make_async_remote_copy(
            src_ref=src, dst_ref=dst, send_sem=send, recv_sem=recv, device_id=where, device_id_type=MESH
        )

    def wait_bytes(ref, sem):
        pltpu.make_async_copy(ref, ref, sem).wait()

    loads = [
        pltpu.make_async_copy(off_in, off, local_sem.at[0]),
        pltpu.make_async_copy(own_in, own, local_sem.at[1]),
        pltpu.make_async_copy(obj.at[pl.ds(0, 2)], fld.at[pl.ds(0, 2)], local_sem.at[2]),
        pltpu.make_async_copy(obj.at[pl.ds(2, 2)], fld.at[pl.ds(2, 2)], local_sem.at[7]),
        pltpu.make_async_copy(pats_in, pats, local_sem.at[3]),
        pltpu.make_async_copy(probe_in, probe, local_sem.at[4]),
        pltpu.make_async_copy(tab_in, tab, local_sem.at[5]),
        pltpu.make_async_copy(spread_in, spread, local_sem.at[6]),
    ]
    for load in loads:
        load.start()

    barrier = pltpu.get_barrier_semaphore()
    friends = [up, down, left, right]
    friends += [g_peer(j) for j in range(1, ng)]
    friends += [w_peer(j) for j in range(1, nw)]
    for friend in friends:
        pl.semaphore_signal(barrier, inc=1, device_id=friend, device_id_type=MESH)
    def lower(s, j):
        low[s][1 + j] = fld[pl.ds(2 * s, 2), :, pl.ds(j * M, M)].reshape(2 * M, M).astype(BF16)

    for load in loads[:3]:
        load.wait()
    for j in (0, inner - 1):
        lower(0, j)
    pl.semaphore_wait(barrier, len(friends))

    info = [
        remote(off, off_nb.at[0], info_s.at[0], info_r.at[0], down),
        remote(own, own_nb.at[0], info_s.at[1], info_r.at[1], down),
        remote(off, off_nb.at[1], info_s.at[2], info_r.at[2], up),
        remote(own, own_nb.at[1], info_s.at[3], info_r.at[3], up),
    ]
    for copy in info:
        copy.start()
    cols = []
    for s in range(2):
        if s == 1:
            loads[3].wait()
            for j in (0, inner - 1):
                lower(1, j)
        cols.append([
            remote(low[s].at[inner], low[s].at[0], col_s.at[s, 0], col_r.at[s, 0], right),
            remote(low[s].at[1], low[s].at[inner + 1], col_s.at[s, 1], col_r.at[s, 1], left),
        ])
        for copy in cols[s]:
            copy.start()
    for s in range(2):
        for j in range(1, inner - 1):
            lower(s, j)
    sends = info + cols[0] + cols[1]

    firsts = [None] * (3 * MOST)

    def build_sel(k, slot):
        firsts[k] = jnp.minimum(slot[1] // M, inner - 1)
        sel[k] = one_hot(3 * M, W, slot[1] - firsts[k] * M)

    mine = slot_info(lambda n: own[n], lambda n, i: off[i, n], bands, t)
    for k in range(MOST):
        build_sel(MOST + k, mine[k])
        rows_in[k] = (
            lax.broadcasted_iota(jnp.int32, (W, 3 * M), 1)
            == lax.broadcasted_iota(jnp.int32, (W, 3 * M), 0) + mine[k][0]
        ).astype(F32).astype(BF16)
        rows_out[k] = one_hot(3 * M, W, mine[k][0])
    for copy in info:
        copy.wait_recv()
    above = slot_info(lambda n: own_nb[0, n], lambda n, i: off_nb[0, i, n], bands, t)
    below = slot_info(lambda n: own_nb[1, n], lambda n, i: off_nb[1, i, n], bands, t)
    for k in range(MOST):
        build_sel(k, above[k])
        build_sel(2 * MOST + k, below[k])

    def chosen(source, first, k):
        near = jnp.concatenate([source[first], source[first + 1], source[first + 2]], axis=1)
        return dot(near, sel[k]).astype(BF16).reshape(2, M, W)

    def start_halo(h, s, source):
        copies = []
        for way in (ci, 1 - ci):
            for k in range(MOST):
                first = jnp.where(way == 0, firsts[k], firsts[2 * MOST + k])
                halo_send[h, way, s, k] = chosen(source, first, way * (2 * MOST) + k)
            copy = remote(
                halo_send.at[h, way, s], parts.at[h, 2 - 2 * way, s], halo_s.at[h, s, way], halo_r.at[h, s, way],
                {"pos": lax.rem(p + npos - 1 + 2 * way, npos)},
            )
            copy.start()
            copies.append(copy)
        return copies

    def own_columns(h, s, source):
        for k in range(MOST):
            parts[h, 1, s, k] = chosen(source, firsts[MOST + k], MOST + k)

    def window(h, s, k, c):
        stack = jnp.concatenate([parts[h, 0, s, k, c], parts[h, 1, s, k, c], parts[h, 2, s, k, c]], axis=0)
        return dot(rows_in[k], stack)

    halo = []
    for s in range(2):
        for copy in cols[s]:
            copy.wait_recv()
        halo.append(start_halo(0, s, low[s]))
    for s in range(2):
        own_columns(0, s, low[s])
    for load in loads[4:]:
        load.wait()
    for k in range(MOST):
        found = pats[0]
        for n in range(1, bands):
            found = jnp.where(mine[k][2] == n, pats[n], found)
        wanted[k] = found
    for k, slot in enumerate(above + mine + below):
        place[pl.ds(k * W, W), :] = (
            lax.broadcasted_iota(jnp.int32, (W, ntiles * M), 1)
            == lax.broadcasted_iota(jnp.int32, (W, ntiles * M), 0) + slot[1]
        ).astype(F32).astype(BF16)

    def transform(k, way):
        half = dot(x[k], tab[way]).astype(BF16)
        mid[k, pl.ds(0, W)] = half[:, :W]
        mid[k, pl.ds(W, W)] = half[:, W:]
        both = dot(tab[1 - way], mid[k])
        return both[:W], both[W:]

    def put(k, re, im):
        x[k, :, pl.ds(0, W)] = re.astype(BF16)
        x[k, :, pl.ds(W, W)] = im.astype(BF16)

    for it in range(ITERS):
        more = it + 1 < ITERS

        def fold_out(k, s, c, value):
            rows = dot(rows_out[k], value.astype(BF16)).astype(BF16)
            fold_send[it, 0, s, k, c] = rows[:M]
            contrib[it, 1, s, k, c] = rows[M : 2 * M]
            fold_send[it, 1, s, k, c] = rows[2 * M :]

        def start_fold(s):
            copies = []
            for way in (ci, 1 - ci):
                copy = remote(
                    fold_send.at[it, way, s], contrib.at[it, 2 - 2 * way, s],
                    fold_s.at[it, s, way], fold_r.at[it, s, way],
                    {"pos": lax.rem(p + npos - 1 + 2 * way, npos)},
                )
                copy.start()
                copies.append(copy)
            return copies

        def sum_columns(terms, s, j):
            both = dot(terms, place[:, pl.ds(j * M, 2 * M)])
            acc[s, j] = both[:, :M]
            acc[s, j + 1] = both[:, M:]

        def sum_edges(s):
            terms = jnp.concatenate(
                [contrib[it, g, s, k].reshape(2 * M, W) for g in range(3) for k in range(MOST)], axis=1
            )
            copies = []
            for way, (j, where) in enumerate(((0, left), (ntiles - 2, right))):
                sum_columns(terms, s, j)
                tiles = pl.ds(0, 2) if more else pl.ds(way, 1)
                edge_send[it, way, s, tiles] = acc[s, pl.ds(j, 2) if more else pl.ds(j + way, 1)].astype(BF16)
                copy = remote(
                    edge_send.at[it, way, s, tiles], edge_recv.at[it, 1 - way, s, tiles],
                    edge_s.at[it, s, way], edge_r.at[it, s, way], where,
                )
                copy.start()
                copies.append(copy)
            return terms, copies

        def add_edges(s, copies):
            for copy in copies:
                copy.wait_recv()
            for way, j in ((0, 0), (1, ntiles - 2)):
                tiles = pl.ds(0, 2) if more else pl.ds(1 - way, 1)
                place_at = pl.ds(j, 2) if more else pl.ds(j + 1 - way, 1)
                acc[s, place_at] = acc[s, place_at] + edge_recv[it, way, s, tiles].astype(F32)

        def squares(s, j, count):
            values = acc[s, pl.ds(j, count)].reshape(count * 2 * M // 8, 8, M)
            return jnp.sum(values * values, axis=0)

        for copy in halo[0]:
            copy.wait_recv()
        for k in range(MOST):
            for c in range(2):
                found = window(it, 0, k, c)
                patch[k, c] = found if it == 0 else patch[k, c] - scale * found
            re = probe[0] * patch[k, 0] - probe[1] * patch[k, 1]
            im = probe[0] * patch[k, 1] + probe[1] * patch[k, 0]
            put(k, re, im)
        for k in range(MOST):
            a, b = transform(k, 0)
            put(k, spread[0] * a - spread[1] * b, spread[0] * b + spread[1] * a)
        for copy in halo[1]:
            copy.wait_recv()
        for k in range(MOST):
            for c in range(2):
                found = window(it, 1, k, c)
                patch[k, 2 + c] = found if it == 0 else patch[k, 2 + c] - scale * found
        for k in range(MOST):
            a, b = transform(k, 1)
            psi1[k, 0] = a
            psi1[k, 1] = b
            put(k, a * patch[k, 2] - b * patch[k, 3], a * patch[k, 3] + b * patch[k, 2])
        for k in range(MOST):
            a, b = transform(k, 0)
            misfit = jnp.where(mine[k][3] > 0, a * a + b * b - wanted[k], 0.0)
            put(k, misfit * a, misfit * b)

        for k in range(MOST):
            a, b = transform(k, 1)
            put(k, patch[k, 2] * a + patch[k, 3] * b, patch[k, 2] * b - patch[k, 3] * a)
            fold_out(k, 1, 0, psi1[k, 0] * a + psi1[k, 1] * b)
            fold_out(k, 1, 1, psi1[k, 0] * b - psi1[k, 1] * a)
        fold1 = start_fold(1)
        for k in range(MOST):
            a, b = transform(k, 0)
            put(k, spread[0] * a + spread[1] * b, spread[0] * b - spread[1] * a)
        for k in range(MOST):
            a, b = transform(k, 1)
            re = patch[k, 0] * a + patch[k, 1] * b
            im = patch[k, 0] * b - patch[k, 1] * a
            pg[0] = re if k == 0 else pg[0] + re
            pg[1] = im if k == 0 else pg[1] + im
            if k == MOST - 1:
                pair_send[it] = pg[...].astype(BF16)
                halves = remote(pair_send.at[it, 1 - ci], pair.at[it], pair_s.at[it, 0], pair_r.at[it, 0], twin)
                halves.start()
            fold_out(k, 0, 0, probe[0] * a + probe[1] * b)
            fold_out(k, 0, 1, probe[0] * b - probe[1] * a)

        halves.wait_recv()
        rs1_send[it] = (pg[ci] + pair[it].astype(F32)).astype(BF16).reshape(ng, W // ng, W)
        for j in range(1, ng):
            remote(
                rs1_send.at[it, g_index(j)], rs1.at[it, me_g], p_s.at[it, 0], p_r.at[it, 0], g_peer(j)
            ).start()
        fold0 = start_fold(0)
        rs1[it, me_g] = rs1_send[it, me_g]

        if it > 0:
            for s in range(2):
                for j in range(inner):
                    here = (pl.ds(2 * s, 2), slice(None), pl.ds(j * M, M))
                    fld[here] = fld[here] - scale * acc[s, 1 + j].reshape(2, M, M)
        for copy in fold1:
            copy.wait_recv()
        terms, edge1 = sum_edges(1)
        for j in range(2, ntiles - 2, 2):
            sum_columns(terms, 1, j)

        wait_bytes(rs1.at[it, pl.ds(0, ng - 1)], p_r.at[it, 0])
        rs2_send[it] = jnp.sum(rs1[it].astype(F32), axis=0).astype(BF16)
        for j in range(1, nz):
            remote(rs2_send.at[it], rs2.at[it, zi], p_s.at[it, 1], p_r.at[it, 1], z_peer(j)).start()
        rs2[it, zi] = rs2_send[it]

        for copy in fold0:
            copy.wait_recv()
        terms, edge0 = sum_edges(0)

        sends += fold0 + fold1 + edge0 + edge1 + halo[0] + halo[1]
        halo = [None, None]
        if nz > 1:
            wait_bytes(rs2.at[it, pl.ds(0, nz - 1)], p_r.at[it, 1])
        ag[it, ci, me_g] = jnp.sum(rs2[it].astype(F32), axis=0).astype(BF16)
        for j in range(1, ng):
            remote(
                ag.at[it, ci, me_g], ag.at[it, ci, me_g], p_s.at[it, 2], p_r.at[it, 2], g_peer(j)
            ).start()

        add_edges(1, edge1)
        if more:
            steps[1] = acc[1].astype(BF16)
            halo[1] = start_halo(it + 1, 1, steps.at[1])
        for j in range(2, ntiles - 2, 2):
            sum_columns(terms, 0, j)
        total = squares(1, 1, inner) + squares(0, 2, inner - 2)
        add_edges(0, edge0)
        sq_send[it, 0] = jnp.sum(total + squares(0, 1, 1) + squares(0, inner, 1), axis=0, keepdims=True)
        both = remote(sq_send.at[it, 0], sq_send.at[it, 1], pair_s.at[it, 2], pair_r.at[it, 2], twin)
        both.start()
        if more:
            steps[0] = acc[0].astype(BF16)
        both.wait_recv()
        sends += [both]
        sq_send[it, 2] = sq_send[it, 0] + sq_send[it, 1]
        for j in range(1, chips):
            remote(sq_send.at[it, 2], sq_all.at[it, me], q_s.at[it], q_r.at[it], chip_peer(j)).start()
        sq_all[it, me] = sq_send[it, 2]
        if more:
            halo[0] = start_halo(it + 1, 0, steps.at[0])

        wait_bytes(rs1.at[it, pl.ds(0, ng - 1)], p_r.at[it, 2])
        whole = remote(ag.at[it, ci], ag.at[it, ci], pair_s.at[it, 1], pair_r.at[it, 1], twin)
        whole.start()
        if more:
            for s in range(2):
                own_columns(it + 1, s, steps.at[s])
        whole.wait_recv()
        sends += [halves, whole]
        grad = ag[it].astype(F32).reshape(2, W, W)
        mean = jnp.sum(grad * grad) / float(2 * W * W)
        probe[...] = probe[...] - ETA_PROBE * lax.rsqrt(mean + 1e-06) * grad

        wait_bytes(sq_all.at[it, pl.ds(0, chips - 1)], q_r.at[it])
        mean = jnp.sum(jnp.sum(sq_all[it], axis=0)) / cells
        scale = ETA_OBJECT * lax.rsqrt(mean + 1e-06)

    for s in range(2):
        for j in range(inner):
            here = (pl.ds(2 * s, 2), slice(None), pl.ds(j * M, M))
            obj_out[here] = fld[here] - scale * acc[s, 1 + j].reshape(2, M, M)
    probe_out[...] = probe[...]
    for copy in sends:
        copy.wait_send()
    for it in range(ITERS):
        wait_bytes(rs1.at[it, pl.ds(0, ng - 1)], p_s.at[it, 0])
        if nz > 1:
            wait_bytes(rs2.at[it, pl.ds(0, nz - 1)], p_s.at[it, 1])
        wait_bytes(rs1.at[it, pl.ds(0, ng - 1)], p_s.at[it, 2])
        wait_bytes(sq_all.at[it, pl.ds(0, chips - 1)], q_s.at[it])


def per_device(object_slices, probe, patterns, offsets, owner):
    nslice, _, rows, cols = object_slices.shape
    bands = patterns.shape[0]
    npos, ntile = lax.axis_size("pos"), lax.axis_size("tile")
    nw = 8 if npos % 8 == 0 else 2
    ng = npos // nw * ntile
    ntiles = cols // M + 2
    cells = float(nslice * 2 * rows * cols * npos * ntile)
    dft, spread = tables()
    vmem, dma = pltpu.VMEM, pltpu.SemaphoreType.DMA
    any_space = pl.BlockSpec(memory_space=pl.ANY)
    scratch = [
        pltpu.SMEM((2, bands), jnp.int32),
        pltpu.SMEM((bands,), jnp.int32),
        pltpu.SMEM((2, 2, bands), jnp.int32),
        pltpu.SMEM((2, bands), jnp.int32),
        vmem((4, M, cols), F32),
        vmem((2, ntiles, 2 * M, M), F32),
        vmem((ntiles, 2 * M, M), BF16),
        vmem((ntiles, 2 * M, M), BF16),
        vmem((2, ntiles, 2 * M, M), BF16),
        vmem((ITERS, 3, 2, MOST, 2, M, W), BF16),
        vmem((ITERS, 2, 2, MOST, 2, M, W), BF16),
        vmem((ITERS, 2, 2, MOST, 2, M, W), BF16),
        vmem((ITERS, 3, 2, MOST, 2, M, W), BF16),
        vmem((ITERS, 2, 2, 2, 2 * M, M), BF16),
        vmem((ITERS, 2, 2, 2, 2 * M, M), BF16),
        vmem((2, W, W), F32),
        vmem((bands, W, W), F32),
        vmem((MOST, W, W), F32),
        vmem((2, 2 * W, 2 * W), BF16),
        vmem((2, W, W), F32),
        vmem((3 * MOST, 3 * M, W), BF16),
        vmem((3 * MOST * W, ntiles * M), BF16),
        vmem((MOST, W, 3 * M), BF16),
        vmem((MOST, 3 * M, W), BF16),
        vmem((MOST, 4, W, W), F32),
        vmem((MOST, W, 2 * W), BF16),
        vmem((MOST, 2 * W, W), BF16),
        vmem((MOST, 2, W, W), F32),
        vmem((2, W, W), F32),
        vmem((ITERS, 2, W, W), BF16),
        vmem((ITERS, W, W), BF16),
        vmem((ITERS, ng, W // ng, W), BF16),
        vmem((ITERS, ng, W // ng, W), BF16),
        vmem((ITERS, W // ng, W), BF16),
        vmem((ITERS, nw // 2, W // ng, W), BF16),
        vmem((ITERS, 2, ng, W // ng, W), BF16),
        vmem((ITERS, npos // 2 * ntile, 1, M), F32),
        vmem((ITERS, 3, 1, M), F32),
        dma((8,)),
        dma((4,)), dma((4,)),
        dma((2, 2)), dma((2, 2)),
        dma((ITERS, 2, 2)), dma((ITERS, 2, 2)),
        dma((ITERS, 2, 2)), dma((ITERS, 2, 2)),
        dma((ITERS, 2, 2)), dma((ITERS, 2, 2)),
        dma((ITERS, 3)), dma((ITERS, 3)),
        dma((ITERS,)), dma((ITERS,)),
        dma((ITERS, 3)), dma((ITERS, 3)),
    ]
    operands = (
        offsets.T,
        owner,
        object_slices.reshape(4, rows, cols),
        probe,
        patterns,
        jnp.asarray(dft),
        jnp.asarray(spread),
    )
    field, current = pl.pallas_call(
        functools.partial(body, (npos, ntile, nw, bands, cols, cells)),
        out_shape=(pltpu.VMEM((4, rows, cols), F32), pltpu.VMEM((2, W, W), F32)),
        in_specs=[any_space] * 7,
        out_specs=(pl.BlockSpec(memory_space=pltpu.VMEM),) * 2,
        scratch_shapes=scratch,
        compiler_params=pltpu.CompilerParams(
            collective_id=0, has_side_effects=True, vmem_limit_bytes=48 * 1024 * 1024
        ),
    )(*(pltpu.with_memory_space_constraint(operand, pltpu.HBM) for operand in operands))
    return field.reshape(nslice, 2, rows, cols), current


def solution(mesh):
    return jax.shard_map(
        per_device,
        mesh=mesh,
        in_specs=(
            P(None, None, "pos", "tile"),
            P(),
            P("pos", None, None),
            P("pos", None),
            P("pos"),
        ),
        out_specs=(P(None, None, "pos", "tile"), P()),
        check_vma=False,
    )
```

```python
import functools
import math

import jax
import jax.numpy as jnp
import numpy as np
from jax import lax
from jax.experimental import pallas as pl
from jax.experimental.pallas import tpu as pltpu
from jax.sharding import PartitionSpec as P

ITERS = 2
MOST = 2
FRESNEL = 0.05
ETA_OBJECT = 0.5
ETA_PROBE = 0.5
W = 256
M = 128
MESH = pl.DeviceIdType.MESH
F32 = jnp.float32
BF16 = jnp.bfloat16


def tables():
    indices = np.arange(W)
    angles = (indices[:, None] * indices[None, :] % W) * (2.0 * math.pi / W)
    cosine = np.cos(angles) / math.sqrt(W)
    sine = np.sin(angles) / math.sqrt(W)
    ahead = np.block([[cosine, -sine], [sine, cosine]])
    behind = np.block([[cosine, sine], [-sine, cosine]])
    dft = np.stack([ahead, behind]).astype(np.float32).astype(jnp.bfloat16)
    frequency = ((indices + W // 2) % W - W // 2).astype(np.float32)
    phases = -math.pi * FRESNEL / W * (frequency[:, None] ** 2 + frequency[None, :] ** 2)
    spread = np.stack([np.cos(phases), np.sin(phases)]).astype(np.float32)
    return dft, spread


def slot_info(owner_of, offset_of, bands, tile):
    zero = jnp.int32(0)
    found = zero
    slots = [[zero, zero, zero, zero] for _ in range(MOST)]
    for n in range(bands):
        live = owner_of(n) == tile
        row, col = offset_of(n, 0) + M, offset_of(n, 1) + M
        for k in range(MOST):
            here = jnp.logical_and(live, found == k)
            slots[k] = [
                jnp.where(here, new, old)
                for new, old in zip((row, col, jnp.int32(n), jnp.int32(1)), slots[k])
            ]
        found = found + live.astype(jnp.int32)
    return slots


def one_hot(rows, cols, shift):
    row = lax.broadcasted_iota(jnp.int32, (rows, cols), 0)
    col = lax.broadcasted_iota(jnp.int32, (rows, cols), 1)
    return (row == col + shift).astype(F32).astype(BF16)


def dot(a, b):
    return jnp.dot(a, b, preferred_element_type=F32)


def body(sizes, *refs):
    (npos, ntile, nw, bands, block_cols, cells) = sizes
    (off_in, own_in, obj, probe_in, pats_in, tab_in, spread_in, obj_out, probe_out) = refs[:9]
    (
        off, own, off_nb, own_nb, fld, acc, low0, low1, steps, parts, halo_send, fold_send, contrib, edge_send, edge_recv,
        probe, pats, wanted, tab, spread, sel, place, rows_in, rows_out, patch, x, mid, psi1, pg,
        pair_send, pair, rs1_send, rs1, rs2_send, rs2, ag, sq_all, sq_send,
        local_sem, info_s, info_r, col_s, col_r, halo_s, halo_r, fold_s, fold_r, edge_s, edge_r,
        p_s, p_r, q_s, q_r, pair_s, pair_r,
    ) = refs[9:]
    inner = block_cols // M
    low = (low0, low1)
    ntiles = inner + 2
    nx = npos // nw
    ng = nx * ntile
    nz = nw // 2
    p = lax.axis_index("pos")
    t = lax.axis_index("tile")
    xi, wi = p // nw, p % nw
    zi, ci = wi // 2, wi % 2
    me_g = xi * ntile + t
    chips = npos // 2 * ntile
    me = p // 2 * ntile + t

    up = {"pos": lax.rem(p + npos - 1, npos)}
    down = {"pos": lax.rem(p + 1, npos)}
    left = {"tile": lax.rem(t + ntile - 1, ntile)}
    right = {"tile": lax.rem(t + 1, ntile)}

    def g_peer(j):
        return {
            "pos": lax.rem(xi + j // ntile, nx) * nw + wi,
            "tile": lax.rem(t + j % ntile, ntile),
        }

    def g_index(j):
        return lax.rem(xi + j // ntile, nx) * ntile + lax.rem(t + j % ntile, ntile)

    def w_peer(j):
        return {"pos": xi * nw + lax.rem(wi + j, nw)}

    def z_peer(j):
        return {"pos": xi * nw + lax.rem(zi + j, nz) * 2 + ci}

    twin = {"pos": xi * nw + zi * 2 + 1 - ci}

    def chip_peer(j):
        return {"pos": lax.rem(p + j // ntile * 2, npos), "tile": lax.rem(t + j % ntile, ntile)}

    def remote(src, dst, send, recv, where):
        return pltpu.make_async_remote_copy(
            src_ref=src, dst_ref=dst, send_sem=send, recv_sem=recv, device_id=where, device_id_type=MESH
        )

    def wait_bytes(ref, sem):
        pltpu.make_async_copy(ref, ref, sem).wait()

    loads = [
        pltpu.make_async_copy(off_in, off, local_sem.at[0]),
        pltpu.make_async_copy(own_in, own, local_sem.at[1]),
        pltpu.make_async_copy(obj.at[pl.ds(0, 2)], fld.at[pl.ds(0, 2)], local_sem.at[2]),
        pltpu.make_async_copy(obj.at[pl.ds(2, 2)], fld.at[pl.ds(2, 2)], local_sem.at[7]),
        pltpu.make_async_copy(pats_in, pats, local_sem.at[3]),
        pltpu.make_async_copy(probe_in, probe, local_sem.at[4]),
        pltpu.make_async_copy(tab_in, tab, local_sem.at[5]),
        pltpu.make_async_copy(spread_in, spread, local_sem.at[6]),
    ]
    for load in loads:
        load.start()

    barrier = pltpu.get_barrier_semaphore()
    friends = [up, down, left, right]
    friends += [g_peer(j) for j in range(1, ng)]
    friends += [w_peer(j) for j in range(1, nw)]
    for friend in friends:
        pl.semaphore_signal(barrier, inc=1, device_id=friend, device_id_type=MESH)
    def lower(s, j):
        low[s][1 + j] = fld[pl.ds(2 * s, 2), :, pl.ds(j * M, M)].reshape(2 * M, M).astype(BF16)

    for load in loads[:3]:
        load.wait()
    for j in (0, inner - 1):
        lower(0, j)
    pl.semaphore_wait(barrier, len(friends))

    info = [
        remote(off, off_nb.at[0], info_s.at[0], info_r.at[0], down),
        remote(own, own_nb.at[0], info_s.at[1], info_r.at[1], down),
        remote(off, off_nb.at[1], info_s.at[2], info_r.at[2], up),
        remote(own, own_nb.at[1], info_s.at[3], info_r.at[3], up),
    ]
    for copy in info:
        copy.start()
    cols = []
    for s in range(2):
        if s == 1:
            loads[3].wait()
            for j in (0, inner - 1):
                lower(1, j)
        cols.append([
            remote(low[s].at[inner], low[s].at[0], col_s.at[s, 0], col_r.at[s, 0], right),
            remote(low[s].at[1], low[s].at[inner + 1], col_s.at[s, 1], col_r.at[s, 1], left),
        ])
        for copy in cols[s]:
            copy.start()
    for s in range(2):
        for j in range(1, inner - 1):
            lower(s, j)
    sends = info + cols[0] + cols[1]

    firsts = [None] * (3 * MOST)

    def build_sel(k, slot):
        firsts[k] = jnp.minimum(slot[1] // M, inner - 1)
        sel[k] = one_hot(3 * M, W, slot[1] - firsts[k] * M)

    mine = slot_info(lambda n: own[n], lambda n, i: off[i, n], bands, t)
    for k in range(MOST):
        build_sel(MOST + k, mine[k])
        rows_in[k] = (
            lax.broadcasted_iota(jnp.int32, (W, 3 * M), 1)
            == lax.broadcasted_iota(jnp.int32, (W, 3 * M), 0) + mine[k][0]
        ).astype(F32).astype(BF16)
        rows_out[k] = one_hot(3 * M, W, mine[k][0])
    for copy in info:
        copy.wait_recv()
    above = slot_info(lambda n: own_nb[0, n], lambda n, i: off_nb[0, i, n], bands, t)
    below = slot_info(lambda n: own_nb[1, n], lambda n, i: off_nb[1, i, n], bands, t)
    for k in range(MOST):
        build_sel(k, above[k])
        build_sel(2 * MOST + k, below[k])

    def chosen(source, first, k):
        near = jnp.concatenate([source[first], source[first + 1], source[first + 2]], axis=1)
        return dot(near, sel[k]).astype(BF16).reshape(2, M, W)

    def start_halo(h, s, source, first_of_all=None):
        copies = []
        for way in (ci, 1 - ci):
            for k in range(MOST):
                first = jnp.where(way == 0, firsts[k], firsts[2 * MOST + k])
                halo_send[h, way, s, k] = chosen(source, first, way * (2 * MOST) + k)
            if first_of_all is not None:
                first_of_all()
                first_of_all = None
            copy = remote(
                halo_send.at[h, way, s], parts.at[h, 2 - 2 * way, s], halo_s.at[h, s, way], halo_r.at[h, s, way],
                {"pos": lax.rem(p + npos - 1 + 2 * way, npos)},
            )
            copy.start()
            copies.append(copy)
        return copies

    def own_columns(h, s, source):
        for k in range(MOST):
            parts[h, 1, s, k] = chosen(source, firsts[MOST + k], MOST + k)

    def window(h, s, k, c):
        stack = jnp.concatenate([parts[h, 0, s, k, c], parts[h, 1, s, k, c], parts[h, 2, s, k, c]], axis=0)
        return dot(rows_in[k], stack)

    halo = []
    for s in range(2):
        for copy in cols[s]:
            copy.wait_recv()
        halo.append(start_halo(0, s, low[s]))
    for s in range(2):
        own_columns(0, s, low[s])
    for load in loads[4:]:
        load.wait()
    for k in range(MOST):
        found = pats[0]
        for n in range(1, bands):
            found = jnp.where(mine[k][2] == n, pats[n], found)
        wanted[k] = found
    for k, slot in enumerate(above + mine + below):
        place[pl.ds(k * W, W), :] = (
            lax.broadcasted_iota(jnp.int32, (W, ntiles * M), 1)
            == lax.broadcasted_iota(jnp.int32, (W, ntiles * M), 0) + slot[1]
        ).astype(F32).astype(BF16)

    def transform(k, way):
        half = dot(x[k], tab[way]).astype(BF16)
        mid[k, pl.ds(0, W)] = half[:, :W]
        mid[k, pl.ds(W, W)] = half[:, W:]
        both = dot(tab[1 - way], mid[k])
        return both[:W], both[W:]

    def put(k, re, im):
        x[k, :, pl.ds(0, W)] = re.astype(BF16)
        x[k, :, pl.ds(W, W)] = im.astype(BF16)

    for it in range(ITERS):
        more = it + 1 < ITERS

        def fold_out(k, s, c, value):
            rows = dot(rows_out[k], value.astype(BF16)).astype(BF16)
            fold_send[it, 0, s, k, c] = rows[:M]
            contrib[it, 1, s, k, c] = rows[M : 2 * M]
            fold_send[it, 1, s, k, c] = rows[2 * M :]

        def start_fold(s, k):
            copies = []
            for way in (ci, 1 - ci):
                copy = remote(
                    fold_send.at[it, way, s, k], contrib.at[it, 2 - 2 * way, s, k],
                    fold_s.at[it, s, k, way], fold_r.at[it, s, k, way],
                    {"pos": lax.rem(p + npos - 1 + 2 * way, npos)},
                )
                copy.start()
                copies.append(copy)
            return copies

        def sum_columns(terms, s, j):
            both = dot(terms, place[:, pl.ds(j * M, 2 * M)])
            acc[s, j] = both[:, :M]
            acc[s, j + 1] = both[:, M:]

        def sum_edges(s):
            terms = jnp.concatenate(
                [contrib[it, g, s, k].reshape(2 * M, W) for g in range(3) for k in range(MOST)], axis=1
            )
            copies = []
            for way, (j, where) in enumerate(((0, left), (ntiles - 2, right))):
                sum_columns(terms, s, j)
                tiles = pl.ds(0, 2) if more else pl.ds(way, 1)
                edge_send[it, way, s, tiles] = acc[s, pl.ds(j, 2) if more else pl.ds(j + way, 1)].astype(BF16)
                copy = remote(
                    edge_send.at[it, way, s, tiles], edge_recv.at[it, 1 - way, s, tiles],
                    edge_s.at[it, s, way], edge_r.at[it, s, way], where,
                )
                copy.start()
                copies.append(copy)
            return terms, copies

        def add_edges(s, copies):
            for copy in copies:
                copy.wait_recv()
            for way, j in ((0, 0), (1, ntiles - 2)):
                tiles = pl.ds(0, 2) if more else pl.ds(1 - way, 1)
                place_at = pl.ds(j, 2) if more else pl.ds(j + 1 - way, 1)
                acc[s, place_at] = acc[s, place_at] + edge_recv[it, way, s, tiles].astype(F32)

        def squares(s, j, count):
            values = acc[s, pl.ds(j, count)].reshape(count * 2 * M // 8, 8, M)
            return jnp.sum(values * values, axis=0)

        for copy in halo[0]:
            copy.wait_recv()
        for k in range(MOST):
            for c in range(2):
                found = window(it, 0, k, c)
                patch[k, c] = found if it == 0 else patch[k, c] - scale * found
            re = probe[0] * patch[k, 0] - probe[1] * patch[k, 1]
            im = probe[0] * patch[k, 1] + probe[1] * patch[k, 0]
            put(k, re, im)
        for k in range(MOST):
            a, b = transform(k, 0)
            put(k, spread[0] * a - spread[1] * b, spread[0] * b + spread[1] * a)
        for copy in halo[1]:
            copy.wait_recv()
        for k in range(MOST):
            for c in range(2):
                found = window(it, 1, k, c)
                patch[k, 2 + c] = found if it == 0 else patch[k, 2 + c] - scale * found
        for k in range(MOST):
            a, b = transform(k, 1)
            psi1[k, 0] = a
            psi1[k, 1] = b
            put(k, a * patch[k, 2] - b * patch[k, 3], a * patch[k, 3] + b * patch[k, 2])
        for k in range(MOST):
            a, b = transform(k, 0)
            misfit = jnp.where(mine[k][3] > 0, a * a + b * b - wanted[k], 0.0)
            put(k, misfit * a, misfit * b)

        for k in range(MOST):
            a, b = transform(k, 1)
            put(k, patch[k, 2] * a + patch[k, 3] * b, patch[k, 2] * b - patch[k, 3] * a)
            fold_out(k, 1, 0, psi1[k, 0] * a + psi1[k, 1] * b)
            fold_out(k, 1, 1, psi1[k, 0] * b - psi1[k, 1] * a)
            fold1 = start_fold(1, k) + (fold1 if k > 0 else [])
        for k in range(MOST):
            a, b = transform(k, 0)
            put(k, spread[0] * a + spread[1] * b, spread[0] * b - spread[1] * a)
        for k in range(MOST):
            a, b = transform(k, 1)
            re = patch[k, 0] * a + patch[k, 1] * b
            im = patch[k, 0] * b - patch[k, 1] * a
            pg[0] = re if k == 0 else pg[0] + re
            pg[1] = im if k == 0 else pg[1] + im
            if k == MOST - 1:
                pair_send[it] = pg[...].astype(BF16)
                halves = remote(pair_send.at[it, 1 - ci], pair.at[it], pair_s.at[it, 0], pair_r.at[it, 0], twin)
                halves.start()
            fold_out(k, 0, 0, probe[0] * a + probe[1] * b)
            fold_out(k, 0, 1, probe[0] * b - probe[1] * a)
            if k == 0:
                fold0 = start_fold(0, 0)

        halves.wait_recv()
        rs1_send[it] = (pg[ci] + pair[it].astype(F32)).astype(BF16).reshape(ng, W // ng, W)
        for j in range(1, ng):
            remote(
                rs1_send.at[it, g_index(j)], rs1.at[it, me_g], p_s.at[it, 0], p_r.at[it, 0], g_peer(j)
            ).start()
        fold0 += start_fold(0, 1)
        rs1[it, me_g] = rs1_send[it, me_g]

        if it > 0:
            for s in range(2):
                for j in range(inner):
                    here = (pl.ds(2 * s, 2), slice(None), pl.ds(j * M, M))
                    fld[here] = fld[here] - scale * acc[s, 1 + j].reshape(2, M, M)
        for copy in fold1:
            copy.wait_recv()
        terms, edge1 = sum_edges(1)
        for j in range(2, ntiles - 2, 2):
            sum_columns(terms, 1, j)

        wait_bytes(rs1.at[it, pl.ds(0, ng - 1)], p_r.at[it, 0])
        rs2_send[it] = jnp.sum(rs1[it].astype(F32), axis=0).astype(BF16)
        for j in range(1, nz):
            remote(rs2_send.at[it], rs2.at[it, zi], p_s.at[it, 1], p_r.at[it, 1], z_peer(j)).start()
        rs2[it, zi] = rs2_send[it]

        for copy in fold0:
            copy.wait_recv()
        terms, edge0 = sum_edges(0)

        sends += fold0 + fold1 + edge0 + edge1 + halo[0] + halo[1]
        halo = [None, None]
        if nz > 1:
            wait_bytes(rs2.at[it, pl.ds(0, nz - 1)], p_r.at[it, 1])
        ag[it, ci, me_g] = jnp.sum(rs2[it].astype(F32), axis=0).astype(BF16)
        for j in range(1, ng):
            remote(
                ag.at[it, ci, me_g], ag.at[it, ci, me_g], p_s.at[it, 2], p_r.at[it, 2], g_peer(j)
            ).start()

        add_edges(1, edge1)
        if more:
            steps[1] = acc[1].astype(BF16)
            halo[1] = start_halo(it + 1, 1, steps.at[1])
        for j in range(2, ntiles - 2, 2):
            sum_columns(terms, 0, j)
        total = squares(1, 1, inner) + squares(0, 2, inner - 2)
        add_edges(0, edge0)
        sq_send[it, 0] = jnp.sum(total + squares(0, 1, 1) + squares(0, inner, 1), axis=0, keepdims=True)
        both = remote(sq_send.at[it, 0], sq_send.at[it, 1], pair_s.at[it, 2], pair_r.at[it, 2], twin)
        both.start()
        sends += [both]

        def send_squares():
            both.wait_recv()
            sq_send[it, 2] = sq_send[it, 0] + sq_send[it, 1]
            for j in range(1, chips):
                remote(sq_send.at[it, 2], sq_all.at[it, me], q_s.at[it], q_r.at[it], chip_peer(j)).start()
            sq_all[it, me] = sq_send[it, 2]

        if more:
            steps[0] = acc[0].astype(BF16)
            halo[0] = start_halo(it + 1, 0, steps.at[0], send_squares)
        else:
            send_squares()

        wait_bytes(rs1.at[it, pl.ds(0, ng - 1)], p_r.at[it, 2])
        whole = remote(ag.at[it, ci], ag.at[it, ci], pair_s.at[it, 1], pair_r.at[it, 1], twin)
        whole.start()
        if more:
            for s in range(2):
                own_columns(it + 1, s, steps.at[s])
        whole.wait_recv()
        sends += [halves, whole]
        grad = ag[it].astype(F32).reshape(2, W, W)
        mean = jnp.sum(grad * grad) / float(2 * W * W)
        probe[...] = probe[...] - ETA_PROBE * lax.rsqrt(mean + 1e-06) * grad

        wait_bytes(sq_all.at[it, pl.ds(0, chips - 1)], q_r.at[it])
        mean = jnp.sum(jnp.sum(sq_all[it], axis=0)) / cells
        scale = ETA_OBJECT * lax.rsqrt(mean + 1e-06)

    for s in range(2):
        for j in range(inner):
            here = (pl.ds(2 * s, 2), slice(None), pl.ds(j * M, M))
            obj_out[here] = fld[here] - scale * acc[s, 1 + j].reshape(2, M, M)
    probe_out[...] = probe[...]
    for copy in sends:
        copy.wait_send()
    for it in range(ITERS):
        wait_bytes(rs1.at[it, pl.ds(0, ng - 1)], p_s.at[it, 0])
        if nz > 1:
            wait_bytes(rs2.at[it, pl.ds(0, nz - 1)], p_s.at[it, 1])
        wait_bytes(rs1.at[it, pl.ds(0, ng - 1)], p_s.at[it, 2])
        wait_bytes(sq_all.at[it, pl.ds(0, chips - 1)], q_s.at[it])


def per_device(object_slices, probe, patterns, offsets, owner):
    nslice, _, rows, cols = object_slices.shape
    bands = patterns.shape[0]
    npos, ntile = lax.axis_size("pos"), lax.axis_size("tile")
    nw = 8 if npos % 8 == 0 else 2
    ng = npos // nw * ntile
    ntiles = cols // M + 2
    cells = float(nslice * 2 * rows * cols * npos * ntile)
    dft, spread = tables()
    vmem, dma = pltpu.VMEM, pltpu.SemaphoreType.DMA
    any_space = pl.BlockSpec(memory_space=pl.ANY)
    scratch = [
        pltpu.SMEM((2, bands), jnp.int32),
        pltpu.SMEM((bands,), jnp.int32),
        pltpu.SMEM((2, 2, bands), jnp.int32),
        pltpu.SMEM((2, bands), jnp.int32),
        vmem((4, M, cols), F32),
        vmem((2, ntiles, 2 * M, M), F32),
        vmem((ntiles, 2 * M, M), BF16),
        vmem((ntiles, 2 * M, M), BF16),
        vmem((2, ntiles, 2 * M, M), BF16),
        vmem((ITERS, 3, 2, MOST, 2, M, W), BF16),
        vmem((ITERS, 2, 2, MOST, 2, M, W), BF16),
        vmem((ITERS, 2, 2, MOST, 2, M, W), BF16),
        vmem((ITERS, 3, 2, MOST, 2, M, W), BF16),
        vmem((ITERS, 2, 2, 2, 2 * M, M), BF16),
        vmem((ITERS, 2, 2, 2, 2 * M, M), BF16),
        vmem((2, W, W), F32),
        vmem((bands, W, W), F32),
        vmem((MOST, W, W), F32),
        vmem((2, 2 * W, 2 * W), BF16),
        vmem((2, W, W), F32),
        vmem((3 * MOST, 3 * M, W), BF16),
        vmem((3 * MOST * W, ntiles * M), BF16),
        vmem((MOST, W, 3 * M), BF16),
        vmem((MOST, 3 * M, W), BF16),
        vmem((MOST, 4, W, W), F32),
        vmem((MOST, W, 2 * W), BF16),
        vmem((MOST, 2 * W, W), BF16),
        vmem((MOST, 2, W, W), F32),
        vmem((2, W, W), F32),
        vmem((ITERS, 2, W, W), BF16),
        vmem((ITERS, W, W), BF16),
        vmem((ITERS, ng, W // ng, W), BF16),
        vmem((ITERS, ng, W // ng, W), BF16),
        vmem((ITERS, W // ng, W), BF16),
        vmem((ITERS, nw // 2, W // ng, W), BF16),
        vmem((ITERS, 2, ng, W // ng, W), BF16),
        vmem((ITERS, npos // 2 * ntile, 1, M), F32),
        vmem((ITERS, 3, 1, M), F32),
        dma((8,)),
        dma((4,)), dma((4,)),
        dma((2, 2)), dma((2, 2)),
        dma((ITERS, 2, 2)), dma((ITERS, 2, 2)),
        dma((ITERS, 2, MOST, 2)), dma((ITERS, 2, MOST, 2)),
        dma((ITERS, 2, 2)), dma((ITERS, 2, 2)),
        dma((ITERS, 3)), dma((ITERS, 3)),
        dma((ITERS,)), dma((ITERS,)),
        dma((ITERS, 3)), dma((ITERS, 3)),
    ]
    operands = (
        offsets.T,
        owner,
        object_slices.reshape(4, rows, cols),
        probe,
        patterns,
        jnp.asarray(dft),
        jnp.asarray(spread),
    )
    field, current = pl.pallas_call(
        functools.partial(body, (npos, ntile, nw, bands, cols, cells)),
        out_shape=(pltpu.VMEM((4, rows, cols), F32), pltpu.VMEM((2, W, W), F32)),
        in_specs=[any_space] * 7,
        out_specs=(pl.BlockSpec(memory_space=pltpu.VMEM),) * 2,
        scratch_shapes=scratch,
        compiler_params=pltpu.CompilerParams(
            collective_id=0, has_side_effects=True, vmem_limit_bytes=48 * 1024 * 1024
        ),
    )(*(pltpu.with_memory_space_constraint(operand, pltpu.HBM) for operand in operands))
    return field.reshape(nslice, 2, rows, cols), current


def solution(mesh):
    return jax.shard_map(
        per_device,
        mesh=mesh,
        in_specs=(
            P(None, None, "pos", "tile"),
            P(),
            P("pos", None, None),
            P("pos", None),
            P("pos"),
        ),
        out_specs=(P(None, None, "pos", "tile"), P()),
        check_vma=False,
    )
```

```python
import functools
import math

import jax
import jax.numpy as jnp
import numpy as np
from jax import lax
from jax.experimental import pallas as pl
from jax.experimental.pallas import tpu as pltpu
from jax.sharding import PartitionSpec as P

ITERS = 2
MOST = 2
FRESNEL = 0.05
ETA_OBJECT = 0.5
ETA_PROBE = 0.5
W = 256
M = 128
MESH = pl.DeviceIdType.MESH
F32 = jnp.float32
BF16 = jnp.bfloat16


def tables():
    indices = np.arange(W)
    angles = (indices[:, None] * indices[None, :] % W) * (2.0 * math.pi / W)
    cosine = np.cos(angles) / math.sqrt(W)
    sine = np.sin(angles) / math.sqrt(W)
    ahead = np.block([[cosine, -sine], [sine, cosine]])
    behind = np.block([[cosine, sine], [-sine, cosine]])
    dft = np.stack([ahead, behind]).astype(np.float32).astype(jnp.bfloat16)
    frequency = ((indices + W // 2) % W - W // 2).astype(np.float32)
    phases = -math.pi * FRESNEL / W * (frequency[:, None] ** 2 + frequency[None, :] ** 2)
    spread = np.stack([np.cos(phases), np.sin(phases)]).astype(np.float32)
    return dft, spread


def slot_info(owner_of, offset_of, bands, tile):
    zero = jnp.int32(0)
    found = zero
    slots = [[zero, zero, zero, zero] for _ in range(MOST)]
    for n in range(bands):
        live = owner_of(n) == tile
        row, col = offset_of(n, 0) + M, offset_of(n, 1) + M
        for k in range(MOST):
            here = jnp.logical_and(live, found == k)
            slots[k] = [
                jnp.where(here, new, old)
                for new, old in zip((row, col, jnp.int32(n), jnp.int32(1)), slots[k])
            ]
        found = found + live.astype(jnp.int32)
    return slots


def one_hot(rows, cols, shift):
    row = lax.broadcasted_iota(jnp.int32, (rows, cols), 0)
    col = lax.broadcasted_iota(jnp.int32, (rows, cols), 1)
    return (row == col + shift).astype(F32).astype(BF16)


def dot(a, b):
    return jnp.dot(a, b, preferred_element_type=F32)


def body(sizes, *refs):
    (npos, ntile, nw, bands, block_cols, cells) = sizes
    (off_in, own_in, obj, probe_in, pats_in, tab_in, spread_in, obj_out, probe_out) = refs[:9]
    (
        off, own, off_nb, own_nb, fld, acc, low0, low1, steps, parts, halo_send, fold_send, contrib, edge_send, edge_recv,
        probe, pats, wanted, tab, spread, sel, place, rows_in, rows_out, patch, x, mid, psi1, pg,
        pair_send, pair, rs1_send, rs1, rs2_send, rs2, ag, sq_all, sq_send,
        local_sem, info_s, info_r, col_s, col_r, halo_s, halo_r, fold_s, fold_r, edge_s, edge_r,
        p_s, p_r, q_s, q_r, pair_s, pair_r,
    ) = refs[9:]
    inner = block_cols // M
    low = (low0, low1)
    ntiles = inner + 2
    nx = npos // nw
    ng = nx * ntile
    nz = nw // 2
    p = lax.axis_index("pos")
    t = lax.axis_index("tile")
    xi, wi = p // nw, p % nw
    zi, ci = wi // 2, wi % 2
    me_g = xi * ntile + t
    chips = npos // 2 * ntile
    me = p // 2 * ntile + t

    up = {"pos": lax.rem(p + npos - 1, npos)}
    down = {"pos": lax.rem(p + 1, npos)}
    left = {"tile": lax.rem(t + ntile - 1, ntile)}
    right = {"tile": lax.rem(t + 1, ntile)}

    def g_peer(j):
        return {
            "pos": lax.rem(xi + j // ntile, nx) * nw + wi,
            "tile": lax.rem(t + j % ntile, ntile),
        }

    def g_index(j):
        return lax.rem(xi + j // ntile, nx) * ntile + lax.rem(t + j % ntile, ntile)

    def w_peer(j):
        return {"pos": xi * nw + lax.rem(wi + j, nw)}

    def z_peer(j):
        return {"pos": xi * nw + lax.rem(zi + j, nz) * 2 + ci}

    twin = {"pos": xi * nw + zi * 2 + 1 - ci}

    def chip_peer(j):
        return {"pos": lax.rem(p + j // ntile * 2, npos), "tile": lax.rem(t + j % ntile, ntile)}

    def remote(src, dst, send, recv, where):
        return pltpu.make_async_remote_copy(
            src_ref=src, dst_ref=dst, send_sem=send, recv_sem=recv, device_id=where, device_id_type=MESH
        )

    def wait_bytes(ref, sem):
        pltpu.make_async_copy(ref, ref, sem).wait()

    loads = [
        pltpu.make_async_copy(off_in, off, local_sem.at[0]),
        pltpu.make_async_copy(own_in, own, local_sem.at[1]),
        pltpu.make_async_copy(obj.at[pl.ds(0, 2)], fld.at[pl.ds(0, 2)], local_sem.at[2]),
        pltpu.make_async_copy(obj.at[pl.ds(2, 2)], fld.at[pl.ds(2, 2)], local_sem.at[7]),
        pltpu.make_async_copy(pats_in, pats, local_sem.at[3]),
        pltpu.make_async_copy(probe_in, probe, local_sem.at[4]),
        pltpu.make_async_copy(tab_in, tab, local_sem.at[5]),
        pltpu.make_async_copy(spread_in, spread, local_sem.at[6]),
    ]
    for load in loads:
        load.start()

    barrier = pltpu.get_barrier_semaphore()
    friends = [up, down, left, right]
    friends += [g_peer(j) for j in range(1, ng)]
    friends += [w_peer(j) for j in range(1, nw)]
    for friend in friends:
        pl.semaphore_signal(barrier, inc=1, device_id=friend, device_id_type=MESH)
    def lower(s, j):
        low[s][1 + j] = fld[pl.ds(2 * s, 2), :, pl.ds(j * M, M)].reshape(2 * M, M).astype(BF16)

    for load in loads[:3]:
        load.wait()
    for j in (0, inner - 1):
        lower(0, j)
    pl.semaphore_wait(barrier, len(friends))

    info = [
        remote(off, off_nb.at[0], info_s.at[0], info_r.at[0], down),
        remote(own, own_nb.at[0], info_s.at[1], info_r.at[1], down),
        remote(off, off_nb.at[1], info_s.at[2], info_r.at[2], up),
        remote(own, own_nb.at[1], info_s.at[3], info_r.at[3], up),
    ]
    for copy in info:
        copy.start()
    cols = []
    for s in range(2):
        if s == 1:
            loads[3].wait()
            for j in (0, inner - 1):
                lower(1, j)
        cols.append([
            remote(low[s].at[inner], low[s].at[0], col_s.at[s, 0], col_r.at[s, 0], right),
            remote(low[s].at[1], low[s].at[inner + 1], col_s.at[s, 1], col_r.at[s, 1], left),
        ])
        for copy in cols[s]:
            copy.start()
    for s in range(2):
        for j in range(1, inner - 1):
            lower(s, j)
    sends = info + cols[0] + cols[1]

    firsts = [None] * (3 * MOST)

    def build_sel(k, slot):
        firsts[k] = jnp.minimum(slot[1] // M, inner - 1)
        sel[k] = one_hot(3 * M, W, slot[1] - firsts[k] * M)

    mine = slot_info(lambda n: own[n], lambda n, i: off[i, n], bands, t)
    for k in range(MOST):
        build_sel(MOST + k, mine[k])
        rows_in[k] = (
            lax.broadcasted_iota(jnp.int32, (W, 3 * M), 1)
            == lax.broadcasted_iota(jnp.int32, (W, 3 * M), 0) + mine[k][0]
        ).astype(F32).astype(BF16)
        rows_out[k] = one_hot(3 * M, W, mine[k][0])
    for copy in info:
        copy.wait_recv()
    above = slot_info(lambda n: own_nb[0, n], lambda n, i: off_nb[0, i, n], bands, t)
    below = slot_info(lambda n: own_nb[1, n], lambda n, i: off_nb[1, i, n], bands, t)
    for k in range(MOST):
        build_sel(k, above[k])
        build_sel(2 * MOST + k, below[k])

    def chosen(source, first, k):
        near = jnp.concatenate([source[first], source[first + 1], source[first + 2]], axis=1)
        return dot(near, sel[k]).astype(BF16).reshape(2, M, W)

    def start_halo(h, s, source, first_of_all=None):
        copies = []
        for way in (ci, 1 - ci):
            for k in range(MOST):
                first = jnp.where(way == 0, firsts[k], firsts[2 * MOST + k])
                halo_send[h, way, s, k] = chosen(source, first, way * (2 * MOST) + k)
            if first_of_all is not None:
                first_of_all()
                first_of_all = None
            copy = remote(
                halo_send.at[h, way, s], parts.at[h, 2 - 2 * way, s], halo_s.at[h, s, way], halo_r.at[h, s, way],
                {"pos": lax.rem(p + npos - 1 + 2 * way, npos)},
            )
            copy.start()
            copies.append(copy)
        return copies

    def own_columns(h, s, source):
        for k in range(MOST):
            parts[h, 1, s, k] = chosen(source, firsts[MOST + k], MOST + k)

    def window(h, s, k, c):
        stack = jnp.concatenate([parts[h, 0, s, k, c], parts[h, 1, s, k, c], parts[h, 2, s, k, c]], axis=0)
        return dot(rows_in[k], stack)

    halo = []
    for s in range(2):
        for copy in cols[s]:
            copy.wait_recv()
        halo.append(start_halo(0, s, low[s]))
    for s in range(2):
        own_columns(0, s, low[s])
    for load in loads[4:]:
        load.wait()
    for k in range(MOST):
        found = pats[0]
        for n in range(1, bands):
            found = jnp.where(mine[k][2] == n, pats[n], found)
        wanted[k] = found
    for k, slot in enumerate(above + mine + below):
        place[pl.ds(k * W, W), :] = (
            lax.broadcasted_iota(jnp.int32, (W, ntiles * M), 1)
            == lax.broadcasted_iota(jnp.int32, (W, ntiles * M), 0) + slot[1]
        ).astype(F32).astype(BF16)

    def transform(k, way):
        half = dot(x[k], tab[way]).astype(BF16)
        mid[k, pl.ds(0, W)] = half[:, :W]
        mid[k, pl.ds(W, W)] = half[:, W:]
        both = dot(tab[1 - way], mid[k])
        return both[:W], both[W:]

    def put(k, re, im):
        x[k, :, pl.ds(0, W)] = re.astype(BF16)
        x[k, :, pl.ds(W, W)] = im.astype(BF16)

    for it in range(ITERS):
        more = it + 1 < ITERS

        def fold_out(k, s, c, value):
            rows = dot(rows_out[k], value.astype(BF16)).astype(BF16)
            fold_send[it, 0, s, k, c] = rows[:M]
            contrib[it, 1, s, k, c] = rows[M : 2 * M]
            fold_send[it, 1, s, k, c] = rows[2 * M :]

        def start_fold(s, k):
            copies = []
            for way in (ci, 1 - ci):
                copy = remote(
                    fold_send.at[it, way, s, k], contrib.at[it, 2 - 2 * way, s, k],
                    fold_s.at[it, s, k, way], fold_r.at[it, s, k, way],
                    {"pos": lax.rem(p + npos - 1 + 2 * way, npos)},
                )
                copy.start()
                copies.append(copy)
            return copies

        def sum_columns(terms, s, j):
            both = dot(terms, place[:, pl.ds(j * M, 2 * M)])
            acc[s, j] = both[:, :M]
            acc[s, j + 1] = both[:, M:]

        def sum_edges(s):
            terms = jnp.concatenate(
                [contrib[it, g, s, k].reshape(2 * M, W) for g in range(3) for k in range(MOST)], axis=1
            )
            copies = []
            for way, (j, where) in enumerate(((0, left), (ntiles - 2, right))):
                sum_columns(terms, s, j)
                tiles = pl.ds(0, 2) if more else pl.ds(way, 1)
                edge_send[it, way, s, tiles] = acc[s, pl.ds(j, 2) if more else pl.ds(j + way, 1)].astype(BF16)
                copy = remote(
                    edge_send.at[it, way, s, tiles], edge_recv.at[it, 1 - way, s, tiles],
                    edge_s.at[it, s, way], edge_r.at[it, s, way], where,
                )
                copy.start()
                copies.append(copy)
            return terms, copies

        def add_edges(s, copies):
            for copy in copies:
                copy.wait_recv()
            for way, j in ((0, 0), (1, ntiles - 2)):
                tiles = pl.ds(0, 2) if more else pl.ds(1 - way, 1)
                place_at = pl.ds(j, 2) if more else pl.ds(j + 1 - way, 1)
                acc[s, place_at] = acc[s, place_at] + edge_recv[it, way, s, tiles].astype(F32)

        def squares(s, j, count):
            values = acc[s, pl.ds(j, count)].reshape(count * 2 * M // 8, 8, M)
            return jnp.sum(values * values, axis=0)

        for copy in halo[0]:
            copy.wait_recv()
        for k in range(MOST):
            for c in range(2):
                found = window(it, 0, k, c)
                patch[k, c] = found if it == 0 else patch[k, c] - scale * found
            re = probe[0] * patch[k, 0] - probe[1] * patch[k, 1]
            im = probe[0] * patch[k, 1] + probe[1] * patch[k, 0]
            put(k, re, im)
        for k in range(MOST):
            a, b = transform(k, 0)
            put(k, spread[0] * a - spread[1] * b, spread[0] * b + spread[1] * a)
        for copy in halo[1]:
            copy.wait_recv()
        for k in range(MOST):
            for c in range(2):
                found = window(it, 1, k, c)
                patch[k, 2 + c] = found if it == 0 else patch[k, 2 + c] - scale * found
        for k in range(MOST):
            a, b = transform(k, 1)
            psi1[k, 0] = a
            psi1[k, 1] = b
            put(k, a * patch[k, 2] - b * patch[k, 3], a * patch[k, 3] + b * patch[k, 2])
        for k in range(MOST):
            a, b = transform(k, 0)
            misfit = jnp.where(mine[k][3] > 0, a * a + b * b - wanted[k], 0.0)
            put(k, misfit * a, misfit * b)

        for k in range(MOST):
            a, b = transform(k, 1)
            put(k, patch[k, 2] * a + patch[k, 3] * b, patch[k, 2] * b - patch[k, 3] * a)
            fold_out(k, 1, 0, psi1[k, 0] * a + psi1[k, 1] * b)
            fold_out(k, 1, 1, psi1[k, 0] * b - psi1[k, 1] * a)
            fold1 = start_fold(1, k) + (fold1 if k > 0 else [])
        for k in range(MOST):
            a, b = transform(k, 0)
            put(k, spread[0] * a + spread[1] * b, spread[0] * b - spread[1] * a)
        for k in range(MOST):
            a, b = transform(k, 1)
            re = patch[k, 0] * a + patch[k, 1] * b
            im = patch[k, 0] * b - patch[k, 1] * a
            pg[0] = re if k == 0 else pg[0] + re
            pg[1] = im if k == 0 else pg[1] + im
            if k == MOST - 1:
                pair_send[it] = pg[...].astype(BF16)
                halves = remote(pair_send.at[it, 1 - ci], pair.at[it], pair_s.at[it, 0], pair_r.at[it, 0], twin)
                halves.start()
            fold_out(k, 0, 0, probe[0] * a + probe[1] * b)
            fold_out(k, 0, 1, probe[0] * b - probe[1] * a)
            if k == 0:
                fold0 = start_fold(0, 0)

        halves.wait_recv()
        rs1_send[it] = (pg[ci] + pair[it].astype(F32)).astype(BF16).reshape(ng, W // ng, W)
        for j in range(1, ng):
            remote(
                rs1_send.at[it, g_index(j)], rs1.at[it, me_g], p_s.at[it, 0], p_r.at[it, 0], g_peer(j)
            ).start()
        fold0 += start_fold(0, 1)
        rs1[it, me_g] = rs1_send[it, me_g]

        if it > 0:
            for s in range(2):
                for j in range(inner):
                    here = (pl.ds(2 * s, 2), slice(None), pl.ds(j * M, M))
                    fld[here] = fld[here] - scale * acc[s, 1 + j].reshape(2, M, M)
        for copy in fold1:
            copy.wait_recv()
        terms, edge1 = sum_edges(1)
        for j in range(2, ntiles - 2, 2):
            sum_columns(terms, 1, j)

        wait_bytes(rs1.at[it, pl.ds(0, ng - 1)], p_r.at[it, 0])
        rs2_send[it] = jnp.sum(rs1[it].astype(F32), axis=0).astype(BF16)
        for j in range(1, nz):
            remote(rs2_send.at[it], rs2.at[it, zi], p_s.at[it, 1], p_r.at[it, 1], z_peer(j)).start()
        rs2[it, zi] = rs2_send[it]

        for copy in fold0:
            copy.wait_recv()
        terms, edge0 = sum_edges(0)
        for j in range(2, ntiles - 2, 2):
            sum_columns(terms, 0, j)

        sends += fold0 + fold1 + edge0 + edge1 + halo[0] + halo[1]
        halo = [None, None]
        if nz > 1:
            wait_bytes(rs2.at[it, pl.ds(0, nz - 1)], p_r.at[it, 1])
        ag[it, ci, me_g] = jnp.sum(rs2[it].astype(F32), axis=0).astype(BF16)
        for j in range(1, ng):
            remote(
                ag.at[it, ci, me_g], ag.at[it, ci, me_g], p_s.at[it, 2], p_r.at[it, 2], g_peer(j)
            ).start()

        add_edges(1, edge1)
        if more:
            steps[1] = acc[1].astype(BF16)
            halo[1] = start_halo(it + 1, 1, steps.at[1])
        total = squares(1, 1, inner) + squares(0, 2, inner - 2)
        add_edges(0, edge0)
        sq_send[it, 0] = jnp.sum(total + squares(0, 1, 1) + squares(0, inner, 1), axis=0, keepdims=True)
        both = remote(sq_send.at[it, 0], sq_send.at[it, 1], pair_s.at[it, 2], pair_r.at[it, 2], twin)
        both.start()
        sends += [both]

        def send_squares():
            both.wait_recv()
            sq_send[it, 2] = sq_send[it, 0] + sq_send[it, 1]
            for j in range(1, chips):
                remote(sq_send.at[it, 2], sq_all.at[it, me], q_s.at[it], q_r.at[it], chip_peer(j)).start()
            sq_all[it, me] = sq_send[it, 2]

        if more:
            steps[0] = acc[0].astype(BF16)
            halo[0] = start_halo(it + 1, 0, steps.at[0], send_squares)
        else:
            send_squares()

        wait_bytes(rs1.at[it, pl.ds(0, ng - 1)], p_r.at[it, 2])
        whole = remote(ag.at[it, ci], ag.at[it, ci], pair_s.at[it, 1], pair_r.at[it, 1], twin)
        whole.start()
        if more:
            for s in range(2):
                own_columns(it + 1, s, steps.at[s])
        whole.wait_recv()
        sends += [halves, whole]
        grad = ag[it].astype(F32).reshape(2, W, W)
        mean = jnp.sum(grad * grad) / float(2 * W * W)
        probe[...] = probe[...] - ETA_PROBE * lax.rsqrt(mean + 1e-06) * grad

        wait_bytes(sq_all.at[it, pl.ds(0, chips - 1)], q_r.at[it])
        mean = jnp.sum(jnp.sum(sq_all[it], axis=0)) / cells
        scale = ETA_OBJECT * lax.rsqrt(mean + 1e-06)

    for s in range(2):
        for j in range(inner):
            here = (pl.ds(2 * s, 2), slice(None), pl.ds(j * M, M))
            obj_out[here] = fld[here] - scale * acc[s, 1 + j].reshape(2, M, M)
    probe_out[...] = probe[...]
    for copy in sends:
        copy.wait_send()
    for it in range(ITERS):
        wait_bytes(rs1.at[it, pl.ds(0, ng - 1)], p_s.at[it, 0])
        if nz > 1:
            wait_bytes(rs2.at[it, pl.ds(0, nz - 1)], p_s.at[it, 1])
        wait_bytes(rs1.at[it, pl.ds(0, ng - 1)], p_s.at[it, 2])
        wait_bytes(sq_all.at[it, pl.ds(0, chips - 1)], q_s.at[it])


def per_device(object_slices, probe, patterns, offsets, owner):
    nslice, _, rows, cols = object_slices.shape
    bands = patterns.shape[0]
    npos, ntile = lax.axis_size("pos"), lax.axis_size("tile")
    nw = 8 if npos % 8 == 0 else 2
    ng = npos // nw * ntile
    ntiles = cols // M + 2
    cells = float(nslice * 2 * rows * cols * npos * ntile)
    dft, spread = tables()
    vmem, dma = pltpu.VMEM, pltpu.SemaphoreType.DMA
    any_space = pl.BlockSpec(memory_space=pl.ANY)
    scratch = [
        pltpu.SMEM((2, bands), jnp.int32),
        pltpu.SMEM((bands,), jnp.int32),
        pltpu.SMEM((2, 2, bands), jnp.int32),
        pltpu.SMEM((2, bands), jnp.int32),
        vmem((4, M, cols), F32),
        vmem((2, ntiles, 2 * M, M), F32),
        vmem((ntiles, 2 * M, M), BF16),
        vmem((ntiles, 2 * M, M), BF16),
        vmem((2, ntiles, 2 * M, M), BF16),
        vmem((ITERS, 3, 2, MOST, 2, M, W), BF16),
        vmem((ITERS, 2, 2, MOST, 2, M, W), BF16),
        vmem((ITERS, 2, 2, MOST, 2, M, W), BF16),
        vmem((ITERS, 3, 2, MOST, 2, M, W), BF16),
        vmem((ITERS, 2, 2, 2, 2 * M, M), BF16),
        vmem((ITERS, 2, 2, 2, 2 * M, M), BF16),
        vmem((2, W, W), F32),
        vmem((bands, W, W), F32),
        vmem((MOST, W, W), F32),
        vmem((2, 2 * W, 2 * W), BF16),
        vmem((2, W, W), F32),
        vmem((3 * MOST, 3 * M, W), BF16),
        vmem((3 * MOST * W, ntiles * M), BF16),
        vmem((MOST, W, 3 * M), BF16),
        vmem((MOST, 3 * M, W), BF16),
        vmem((MOST, 4, W, W), F32),
        vmem((MOST, W, 2 * W), BF16),
        vmem((MOST, 2 * W, W), BF16),
        vmem((MOST, 2, W, W), F32),
        vmem((2, W, W), F32),
        vmem((ITERS, 2, W, W), BF16),
        vmem((ITERS, W, W), BF16),
        vmem((ITERS, ng, W // ng, W), BF16),
        vmem((ITERS, ng, W // ng, W), BF16),
        vmem((ITERS, W // ng, W), BF16),
        vmem((ITERS, nw // 2, W // ng, W), BF16),
        vmem((ITERS, 2, ng, W // ng, W), BF16),
        vmem((ITERS, npos // 2 * ntile, 1, M), F32),
        vmem((ITERS, 3, 1, M), F32),
        dma((8,)),
        dma((4,)), dma((4,)),
        dma((2, 2)), dma((2, 2)),
        dma((ITERS, 2, 2)), dma((ITERS, 2, 2)),
        dma((ITERS, 2, MOST, 2)), dma((ITERS, 2, MOST, 2)),
        dma((ITERS, 2, 2)), dma((ITERS, 2, 2)),
        dma((ITERS, 3)), dma((ITERS, 3)),
        dma((ITERS,)), dma((ITERS,)),
        dma((ITERS, 3)), dma((ITERS, 3)),
    ]
    operands = (
        offsets.T,
        owner,
        object_slices.reshape(4, rows, cols),
        probe,
        patterns,
        jnp.asarray(dft),
        jnp.asarray(spread),
    )
    field, current = pl.pallas_call(
        functools.partial(body, (npos, ntile, nw, bands, cols, cells)),
        out_shape=(pltpu.VMEM((4, rows, cols), F32), pltpu.VMEM((2, W, W), F32)),
        in_specs=[any_space] * 7,
        out_specs=(pl.BlockSpec(memory_space=pltpu.VMEM),) * 2,
        scratch_shapes=scratch,
        compiler_params=pltpu.CompilerParams(
            collective_id=0, has_side_effects=True, vmem_limit_bytes=48 * 1024 * 1024
        ),
    )(*(pltpu.with_memory_space_constraint(operand, pltpu.HBM) for operand in operands))
    return field.reshape(nslice, 2, rows, cols), current


def solution(mesh):
    return jax.shard_map(
        per_device,
        mesh=mesh,
        in_specs=(
            P(None, None, "pos", "tile"),
            P(),
            P("pos", None, None),
            P("pos", None),
            P("pos"),
        ),
        out_specs=(P(None, None, "pos", "tile"), P()),
        check_vma=False,
    )
```
